32 devices in a mesh: af: 4 (over z), gy: 4 (over x, core), gz: 2 (over y).
Axes of the slice: x: 2, y: 2, z: 4, core: 2. Of those that a mesh axis runs over, the one named last changes fastest.
Arguments:
- slab: bfloat16 [512, 16384], P('af', ('gy', 'gz')), may hold values from -4000 to 4000
- block_owner: int32 [4, 2, 4], P('gy', 'gz'), may hold values from 0 to 3, each once within a row
- basis_init: float32 [512, 128], replicated, may hold values from -0.25 to 0.25
Outputs:
- triangle: float32 [512, 512], replicated
- basis: float32 [512, 128], replicated
- core: bfloat16 [128, 16384], P(None, ('gy', 'gz', 'af'))
The draws below stay inside these ranges and needn't reach their ends.
Inputs may be any that keep to these rules, and one draw needn't show every extreme that they name: For every gy and gz index, block_owner[gy, gz, :] is a permutation of the 4 af indices.
All inputs are finite; a program needn't handle non-finite values.
Results may differ from the reference program's by a relative error of at most 0.0049.
Values may be sent and summed in bfloat16 or wider, within the bound.
No kernel may reach another device: no remote copies, remote signals or barrier semaphores. Data moves between devices by JAX's collectives and lax.ppermute only.
A program may use at most 64 MiB of HBM per device.

```python
import math
import jax
import jax.numpy as jnp
from jax import lax

ROWS = 512
RANK = 128
CDEV = 512
ITERS = 2
AF_DEVS = 4
GY_DEVS = 4
GZ_DEVS = 2
COLS = 16384


def draw_slab(key, part):
    base = jax.random.fold_in(key, 11)
    key_mix, key_rows, key_noise, key_cols, key_coef = jax.random.split(base, 5)
    decay = jnp.exp(-math.log(2.0) * jnp.arange(ROWS, dtype=jnp.float32) / ROWS)
    mixing = (jnp.eye(ROWS, dtype=jnp.float32) + 0.3 * jax.random.normal(key_mix, (ROWS, ROWS), jnp.float32) / math.sqrt(ROWS)) * decay[None, :]
    position = jnp.arange(COLS, dtype=jnp.float32) / COLS
    row_scale = jnp.exp(jax.random.uniform(key_rows, (ROWS, 1), jnp.float32, 0.0, math.log(10.0)))
    coef = jax.random.truncated_normal(key_coef, -4.0, 4.0, (ROWS, COLS), jnp.float32)
    noise = 0.05 * jax.random.truncated_normal(key_noise, -4.0, 4.0, (ROWS, COLS), jnp.float32)
    rising = jnp.exp(math.log(3.0) * position)
    col_scale = jnp.exp(jax.random.uniform(key_cols, (COLS,), jnp.float32, 0.0, math.log(3.5))) * rising
    mixed = jnp.dot(mixing, coef, precision=lax.Precision.HIGHEST)
    values = row_scale * (mixed + noise) * col_scale[None, :]
    return values.astype(jnp.bfloat16)


def centred(key, shape, width, most, held_as=jnp.bfloat16):
    entries = width * jax.random.normal(key, shape, jnp.float32)
    return jnp.clip(entries, min=-most, max=most).astype(held_as)


def setup_inputs(seed: int = 0) -> dict:
    arg_keys = jax.random.split(jax.random.key(seed), 4)
    slab = draw_slab(jax.random.fold_in(arg_keys[3], 71), 0)
    block_owner = jax.vmap(lambda own: jax.random.permutation(own, AF_DEVS))(jax.random.split(arg_keys[1], GY_DEVS * GZ_DEVS)).reshape((GY_DEVS, GZ_DEVS, AF_DEVS)).astype(jnp.int32)
    basis_init = centred(arg_keys[2], (ROWS, RANK), ROWS ** -0.5, 0.25, jnp.float32)
    return dict(slab=slab, block_owner=block_owner, basis_init=basis_init)


exact_mode = lax.Precision.HIGHEST

def orthonormal(matrix):
    inner_prod = jnp.dot(matrix.T, matrix, precision=exact_mode)
    factor = jnp.linalg.cholesky(inner_prod)
    return lax.linalg.triangular_solve(factor, matrix, left_side=False, lower=True, transpose_a=True)

def reference(slab, block_owner, basis_init):
    gram = jnp.dot(slab.astype(jnp.float32), slab.T.astype(jnp.float32), preferred_element_type=jnp.float32) / COLS
    triangle = jnp.linalg.cholesky(gram)
    basis = basis_init
    for sweep in range(ITERS):
        half_basis = orthonormal(jnp.dot(triangle.T, basis, precision=exact_mode))
        basis = orthonormal(jnp.dot(triangle, half_basis, precision=exact_mode))
    narrow = basis.astype(jnp.bfloat16)
    projected = jnp.dot(narrow.T.astype(jnp.float32), slab.astype(jnp.float32), preferred_element_type=jnp.float32).astype(jnp.bfloat16)
    groups = GY_DEVS * GZ_DEVS
    blocks = projected.reshape(RANK, groups, AF_DEVS, CDEV)
    owners = block_owner.reshape(groups, AF_DEVS).astype(jnp.int32)
    source = jnp.argsort(owners, axis=1).astype(jnp.int32)
    index_full = jnp.broadcast_to(source[None, :, :, None], blocks.shape)
    core = jnp.take_along_axis(blocks, index_full, axis=2).reshape(RANK, COLS)
    return (triangle, basis, core)
```

```python
import functools

import jax
import jax.numpy as jnp
from jax import lax
from jax.experimental import pallas as pl
from jax.experimental.pallas import tpu as pltpu
from jax.sharding import PartitionSpec as P

ITERS = 2
GROUP = 16
HIGH = lax.Precision.HIGHEST


def split3(x):
    hi = x.astype(jnp.bfloat16)
    rest = x - hi.astype(jnp.float32)
    mid = rest.astype(jnp.bfloat16)
    low = (rest - mid.astype(jnp.float32)).astype(jnp.bfloat16)
    return hi, mid, low


def dot_nn(a, b):
    return lax.dot_general(a, b, (((1,), (0,)), ((), ())), precision=HIGH, preferred_element_type=jnp.float32)


def dot_nt(a, b):
    return lax.dot_general(a, b, (((1,), (1,)), ((), ())), precision=HIGH, preferred_element_type=jnp.float32)


def dot_tn(a, b):
    return lax.dot_general(a, b, (((0,), (0,)), ((), ())), precision=HIGH, preferred_element_type=jnp.float32)


def eliminate(state, start, n):
    rows = pl.ds(pl.multiple_of(start, GROUP), GROUP)
    left = state[rows, :n]
    right = state[rows, n:]
    shape = (GROUP, n)
    row = lax.broadcasted_iota(jnp.int32, shape, 0)
    lane = lax.broadcasted_iota(jnp.int32, shape, 1)
    cols = [
        jnp.take_along_axis(left, jnp.full(shape, 0, jnp.int32) + (start + k), axis=1, mode="promise_in_bounds")
        for k in range(GROUP)
    ]
    pivots = jnp.ones(shape, jnp.float32)
    for i in range(GROUP):
        pivot = jnp.broadcast_to(cols[i][i : i + 1, :], shape)
        pivots = jnp.where(row == i, pivot, pivots)
        if i == GROUP - 1:
            break
        inverse = 1.0 / pivot
        below = jnp.where(row > i, cols[i], 0.0)
        for k in range(i + 1, GROUP):
            cols[k] = cols[k] - (below * cols[k][i : i + 1, :]) * inverse
        factor = below * inverse
        left = left - factor * left[i : i + 1, :]
        right = right - factor * right[i : i + 1, :]
    scale = lax.rsqrt(pivots)
    left = left * scale
    right = right * scale
    state[rows, :n] = left
    state[rows, n:] = right
    hi, mid, low = split3(jnp.where(lane >= start + GROUP, left, 0.0))
    first = jnp.concatenate([hi, hi, mid, mid, hi, low], axis=0)
    wide = jnp.concatenate([left, right], axis=1)
    hi, mid, low = split3(wide)
    second = jnp.concatenate([hi, mid, hi, mid, low, hi], axis=0)
    delta = lax.dot_general(first, second, (((0,), (0,)), ((), ())), preferred_element_type=jnp.float32)
    state[...] = state[...] - delta


def factor_kernel(gram_ref, basis_ref, cols_ref, tri_ref, out_ref, core_ref, work, one, two):
    size = gram_ref.shape[0]
    n = basis_ref.shape[1]
    phases = size // n
    eye = (
        lax.broadcasted_iota(jnp.int32, (n, n), 0) == lax.broadcasted_iota(jnp.int32, (n, n), 1)
    ).astype(jnp.float32)
    upper = lax.broadcasted_iota(jnp.int32, (n, n), 0) <= lax.broadcasted_iota(jnp.int32, (n, n), 1)
    work[...] = gram_ref[...]
    tri_ref[...] = jnp.zeros_like(tri_ref)
    basis = basis_ref[...]
    for phase in range(max(phases, 2 * ITERS)):
        if phase < phases:
            at = slice(phase * n, (phase + 1) * n)
            rest = slice((phase + 1) * n, size)
            one[:, :n] = work[at, at]
            one[:, n:] = eye
        if phase < 2 * ITERS:
            if phase % 2 == 0:
                wide = dot_nn(gram_ref[...], basis)
                two[:, :n] = dot_tn(basis, wide)
            else:
                two[:, :n] = dot_tn(wide, wide)
            two[:, n:] = eye

        def step(group, carry):
            if phase < phases:
                eliminate(one, group * GROUP, n)
            if phase < 2 * ITERS:
                eliminate(two, group * GROUP, n)
            return carry

        lax.fori_loop(0, n // GROUP, step, 0)
        if phase < phases:
            tri_ref[at, at] = jnp.where(upper, one[:, :n], 0.0).T
            if phase < phases - 1:
                panel = dot_nn(one[:, n:], work[at, rest])
                tri_ref[rest, at] = panel.T
                work[rest, rest] = work[rest, rest] - dot_tn(panel, panel)
        if phase < 2 * ITERS:
            wide = dot_nt(wide, two[:, n:])
            if phase % 2 == 1:
                basis = wide
    out_ref[...] = basis
    narrow = basis.astype(jnp.bfloat16)
    core_ref[...] = lax.dot_general(
        narrow, cols_ref[...], (((0,), (0,)), ((), ())), preferred_element_type=jnp.float32
    ).astype(jnp.bfloat16)


def factor(gram, basis, columns):
    size = gram.shape[0]
    n = basis.shape[1]
    return pl.pallas_call(
        factor_kernel,
        out_shape=(
            jax.ShapeDtypeStruct((size, size), jnp.float32),
            jax.ShapeDtypeStruct((size, n), jnp.float32),
            jax.ShapeDtypeStruct((n, columns.shape[1]), jnp.bfloat16),
        ),
        scratch_shapes=[
            pltpu.VMEM((size, size), jnp.float32),
            pltpu.VMEM((n, 2 * n), jnp.float32),
            pltpu.VMEM((n, 2 * n), jnp.float32),
        ],
        compiler_params=pltpu.CompilerParams(vmem_limit_bytes=32 * 1024 * 1024),
        name="factor",
    )(gram, basis, columns)


def reduce_all(value):
    steps = []
    for axis in ("gy", "gz", "af"):
        distance = 1
        while distance < lax.axis_size(axis):
            steps.append((axis, distance))
            distance *= 2
    rows = value.shape[0]
    cuts = []
    for axis, distance in steps:
        bit = (lax.axis_index(axis) // distance) % 2
        half = value.shape[0] // 2
        kept = lax.dynamic_slice_in_dim(value, bit * half, half, 0)
        sent = lax.dynamic_slice_in_dim(value, (1 - bit) * half, half, 0)
        pairs = [(i, i ^ distance) for i in range(lax.axis_size(axis))]
        value = kept + lax.ppermute(sent, axis, pairs)
        cuts.append((axis, pairs, bit))
    for axis, pairs, bit in reversed(cuts):
        got = lax.ppermute(value, axis, pairs)
        value = jnp.where(
            bit == 0, jnp.concatenate([value, got], 0), jnp.concatenate([got, value], 0)
        )
    return value


def on_device(slab, block_owner, basis_init):
    fibers = lax.axis_size("af")
    local_rows = slab.shape[0]
    block_cols = slab.shape[1] // fibers
    owners = block_owner.reshape(fibers)
    labels = jnp.arange(fibers, dtype=jnp.int32)
    onehot = (owners[:, None] == labels[None, :]).astype(jnp.int32)
    source = jnp.sum(onehot * labels[:, None], axis=0)
    pieces = slab.reshape(local_rows, fibers, block_cols)
    arranged = jnp.take(pieces, source, axis=1)
    received = lax.all_to_all(arranged, "af", split_axis=1, concat_axis=0, tiled=True)
    columns = received.reshape(local_rows * fibers, block_cols)
    devices_all = fibers * lax.axis_size("gy") * lax.axis_size("gz")
    divisor = block_cols * devices_all
    gram_local = (
        lax.dot_general(
            columns, columns, (((1,), (1,)), ((), ())), preferred_element_type=jnp.float32
        )
        / divisor
    )
    summed = reduce_all(gram_local)
    return factor(summed, basis_init, columns)


def solution(mesh):
    placed = (P("af", ("gy", "gz")), P("gy", "gz", None), P())
    return jax.shard_map(
        on_device,
        mesh=mesh,
        in_specs=placed,
        out_specs=(P(), P(), P(None, ("gy", "gz", "af"))),
        check_vma=False,
    )
```

```python
import functools

import jax
import jax.numpy as jnp
import numpy as np
from jax import lax
from jax.experimental import pallas as pl
from jax.experimental.pallas import tpu as pltpu
from jax.sharding import PartitionSpec as P

ITERS = 2
GROUP = 16
HIGH = lax.Precision.HIGHEST


def split3(x):
    hi = x.astype(jnp.bfloat16)
    rest = x - hi.astype(jnp.float32)
    mid = rest.astype(jnp.bfloat16)
    low = (rest - mid.astype(jnp.float32)).astype(jnp.bfloat16)
    return hi, mid, low


def dot_nn(a, b):
    return lax.dot_general(a, b, (((1,), (0,)), ((), ())), precision=HIGH, preferred_element_type=jnp.float32)


def dot_nt(a, b):
    return lax.dot_general(a, b, (((1,), (1,)), ((), ())), precision=HIGH, preferred_element_type=jnp.float32)


def dot_tn(a, b):
    return lax.dot_general(a, b, (((0,), (0,)), ((), ())), precision=HIGH, preferred_element_type=jnp.float32)


def eliminate(state, start, n):
    rows = pl.ds(pl.multiple_of(start, GROUP), GROUP)
    left = state[rows, :n]
    right = state[rows, n:]
    shape = (GROUP, n)
    row = lax.broadcasted_iota(jnp.int32, shape, 0)
    lane = lax.broadcasted_iota(jnp.int32, shape, 1)
    cols = [
        jnp.take_along_axis(left, jnp.full(shape, 0, jnp.int32) + (start + k), axis=1, mode="promise_in_bounds")
        for k in range(GROUP)
    ]
    pivots = jnp.ones(shape, jnp.float32)
    for i in range(GROUP):
        pivot = jnp.broadcast_to(cols[i][i : i + 1, :], shape)
        pivots = jnp.where(row == i, pivot, pivots)
        if i == GROUP - 1:
            break
        inverse = 1.0 / pivot
        below = jnp.where(row > i, cols[i], 0.0)
        for k in range(i + 1, GROUP):
            cols[k] = cols[k] - (below * cols[k][i : i + 1, :]) * inverse
        factor = below * inverse
        left = left - factor * left[i : i + 1, :]
        right = right - factor * right[i : i + 1, :]
    scale = lax.rsqrt(pivots)
    left = left * scale
    right = right * scale
    state[rows, :n] = left
    state[rows, n:] = right
    hi, mid, low = split3(jnp.where(lane >= start + GROUP, left, 0.0))
    first = jnp.concatenate([hi, hi, mid, mid, hi, low], axis=0)
    wide = jnp.concatenate([left, right], axis=1)
    hi, mid, low = split3(wide)
    second = jnp.concatenate([hi, mid, hi, mid, low, hi], axis=0)
    delta = lax.dot_general(first, second, (((0,), (0,)), ((), ())), preferred_element_type=jnp.float32)
    state[...] = state[...] - delta


def upper_blocks(size, n):
    count = size // n
    return [(i, j) for i in range(count) for j in range(i, count)]


def gram_kernel(divisor, n, place_ref, *refs):
    pieces, (columns_ref, gram_ref) = refs[:-2], refs[-2:]
    rows = pieces[0].shape[0]
    for distance, piece in enumerate(pieces):
        start = pl.multiple_of(lax.bitwise_xor(place_ref[0], distance) * rows, rows)
        columns_ref[pl.ds(start, rows), :] = piece[...]
    for b, (i, j) in enumerate(upper_blocks(columns_ref.shape[0], n)):
        gram_ref[b * n : (b + 1) * n, :] = lax.dot_general(
            columns_ref[i * n : (i + 1) * n, :],
            columns_ref[j * n : (j + 1) * n, :],
            (((1,), (1,)), ((), ())),
            preferred_element_type=jnp.float32,
        ) * (1.0 / divisor)


def local_gram(place, pieces, divisor, n):
    rows, width = pieces[0].shape
    size = rows * len(pieces)
    vmem = pl.BlockSpec(memory_space=pltpu.VMEM)
    return pl.pallas_call(
        functools.partial(gram_kernel, divisor, n),
        out_shape=(
            jax.ShapeDtypeStruct((size, width), pieces[0].dtype),
            jax.ShapeDtypeStruct((len(upper_blocks(size, n)) * n, n), jnp.float32),
        ),
        in_specs=[pl.BlockSpec(memory_space=pltpu.SMEM)] + [vmem] * len(pieces),
        out_specs=(vmem, vmem),
        name="local_gram",
    )(place.reshape(1), *pieces)


def factor_kernel(blocks_ref, basis_ref, cols_ref, tri_ref, out_ref, core_ref, gram_ref, work, one, two):
    size = tri_ref.shape[0]
    n = basis_ref.shape[1]
    for b, (i, j) in enumerate(upper_blocks(size, n)):
        block = blocks_ref[b * n : (b + 1) * n, :]
        gram_ref[i * n : (i + 1) * n, j * n : (j + 1) * n] = block
        if i != j:
            gram_ref[j * n : (j + 1) * n, i * n : (i + 1) * n] = block.T
    phases = size // n
    eye = (
        lax.broadcasted_iota(jnp.int32, (n, n), 0) == lax.broadcasted_iota(jnp.int32, (n, n), 1)
    ).astype(jnp.float32)
    upper = lax.broadcasted_iota(jnp.int32, (n, n), 0) <= lax.broadcasted_iota(jnp.int32, (n, n), 1)
    work[...] = gram_ref[...]
    tri_ref[...] = jnp.zeros_like(tri_ref)
    basis = basis_ref[...]
    for phase in range(max(phases, 2 * ITERS)):
        if phase < phases:
            at = slice(phase * n, (phase + 1) * n)
            rest = slice((phase + 1) * n, size)
            one[:, :n] = work[at, at]
            one[:, n:] = eye
        if phase < 2 * ITERS:
            if phase % 2 == 0:
                wide = dot_nn(gram_ref[...], basis)
                two[:, :n] = dot_tn(basis, wide)
            else:
                two[:, :n] = dot_tn(wide, wide)
            two[:, n:] = eye

        def step(group, carry):
            if phase < phases:
                eliminate(one, group * GROUP, n)
            if phase < 2 * ITERS:
                eliminate(two, group * GROUP, n)
            return carry

        lax.fori_loop(0, n // GROUP, step, 0)
        if phase < phases:
            tri_ref[at, at] = jnp.where(upper, one[:, :n], 0.0).T
            if phase < phases - 1:
                panel = dot_nn(one[:, n:], work[at, rest])
                tri_ref[rest, at] = panel.T
                work[rest, rest] = work[rest, rest] - dot_tn(panel, panel)
        if phase < 2 * ITERS:
            wide = dot_nt(wide, two[:, n:])
            if phase % 2 == 1:
                basis = wide
    out_ref[...] = basis
    narrow = basis.astype(jnp.bfloat16)
    core_ref[...] = lax.dot_general(
        narrow, cols_ref[...], (((0,), (0,)), ((), ())), preferred_element_type=jnp.float32
    ).astype(jnp.bfloat16)


def factor(blocks, basis, columns):
    size, n = basis.shape
    return pl.pallas_call(
        factor_kernel,
        out_shape=(
            jax.ShapeDtypeStruct((size, size), jnp.float32),
            jax.ShapeDtypeStruct((size, n), jnp.float32),
            jax.ShapeDtypeStruct((n, columns.shape[1]), jnp.bfloat16),
        ),
        scratch_shapes=[
            pltpu.VMEM((size, size), jnp.float32),
            pltpu.VMEM((size, size), jnp.float32),
            pltpu.VMEM((n, 2 * n), jnp.float32),
            pltpu.VMEM((n, 2 * n), jnp.float32),
        ],
        compiler_params=pltpu.CompilerParams(vmem_limit_bytes=32 * 1024 * 1024),
        name="factor",
    )(blocks, basis, columns)


class Group:
    def __init__(self, bits):
        self.axes = tuple(dict.fromkeys(axis for axis, _ in bits))
        self.bits = bits
        self.size = 2 ** len(bits)
        self.me = 0
        for b, (axis, distance) in enumerate(bits):
            self.me = self.me + (((lax.axis_index(axis) // distance) % 2) << b)

    def swap(self, value, change):
        sizes = [lax.axis_size(axis) for axis in self.axes]
        pairs = []
        for source, place in enumerate(np.ndindex(*sizes)):
            place = list(place)
            for b, (axis, distance) in enumerate(self.bits):
                if (change >> b) & 1:
                    place[self.axes.index(axis)] ^= distance
            pairs.append((source, int(np.ravel_multi_index(place, sizes))))
        return lax.ppermute(value, self.axes, pairs)

    def scatter_sum(self, value):
        part = value.shape[0] // self.size
        got = [
            self.swap(lax.dynamic_slice_in_dim(value, (self.me ^ d) * part, part, 0), d)
            for d in range(1, self.size)
        ]
        return sum(got, lax.dynamic_slice_in_dim(value, self.me * part, part, 0))

    def gather(self, value):
        got = [value] + [self.swap(value, d) for d in range(1, self.size)]
        whole = jnp.zeros((self.size, *value.shape), value.dtype)
        for d in range(self.size):
            whole = lax.dynamic_update_slice_in_dim(whole, got[d][None], self.me ^ d, 0)
        return whole.reshape(self.size * value.shape[0], *value.shape[1:])


def axis_bits(axis):
    size = lax.axis_size(axis)
    assert size & (size - 1) == 0, axis
    return [(axis, 1 << b) for b in range(size.bit_length() - 1)]


def reduce_all(value):
    first, *rest = axis_bits("gy") + axis_bits("gz")
    groups = [Group([first])] + [Group(rest[b : b + 2]) for b in range(0, len(rest), 2)]
    for group in groups:
        value = group.scatter_sum(value)
    for bit in axis_bits("af"):
        value = value + Group([bit]).swap(value, 1)
    for group in reversed(groups):
        value = group.gather(value)
    return value


def on_device(slab, block_owner, basis_init):
    fibers = lax.axis_size("af")
    block_cols = slab.shape[1] // fibers
    owners = block_owner.reshape(fibers)
    labels = jnp.arange(fibers, dtype=jnp.int32)
    onehot = (owners[:, None] == labels[None, :]).astype(jnp.int32)
    source = jnp.sum(onehot * labels[:, None], axis=0)
    along = Group(axis_bits("af"))

    def block_of(distance):
        start = source[along.me ^ distance] * block_cols
        return lax.dynamic_slice_in_dim(slab, start, block_cols, 1)

    pieces = [block_of(0)]
    for distance in range(1, fibers):
        pieces.append(along.swap(block_of(distance), distance))
    devices_all = fibers * lax.axis_size("gy") * lax.axis_size("gz")
    columns, blocks = local_gram(along.me, pieces, block_cols * devices_all, basis_init.shape[1])
    return factor(reduce_all(blocks), basis_init, columns)


def solution(mesh):
    placed = (P("af", ("gy", "gz")), P("gy", "gz", None), P())
    return jax.shard_map(
        on_device,
        mesh=mesh,
        in_specs=placed,
        out_specs=(P(), P(), P(None, ("gy", "gz", "af"))),
        check_vma=False,
    )
```

```python
import functools

import jax
import jax.numpy as jnp
import numpy as np
from jax import lax
from jax.experimental import pallas as pl
from jax.experimental.pallas import tpu as pltpu
from jax.sharding import PartitionSpec as P

ITERS = 2
GROUP = 32
BLOCK = 16
TILE = 8


def split3(x):
    hi = x.astype(jnp.bfloat16)
    rest = x - hi.astype(jnp.float32)
    mid = rest.astype(jnp.bfloat16)
    low = (rest - mid.astype(jnp.float32)).astype(jnp.bfloat16)
    return hi, mid, low


def dot(a, b, dims):
    return lax.dot_general(a, b, (dims, ((), ())), preferred_element_type=jnp.float32)


NN, NT, TN = ((1,), (0,)), ((1,), (1,)), ((0,), (0,))


def deep_dot(a, b, dims):
    (ah, am, al), (bh, bm, bl) = a, b
    left = jnp.concatenate([ah, am, ah, am, ah, al], axis=dims[0][0])
    right = jnp.concatenate([bh, bh, bm, bm, bl, bh], axis=dims[1][0])
    return dot(left, right, dims)


def wide_dot(a, b, dims):
    (ah, am, al), (bh, bm, bl) = a, b
    n = bh.shape[1]
    both = jnp.concatenate([bh, bm], axis=1)
    first = dot(ah, both, dims)
    second = dot(am, both, dims)
    small = dot(
        jnp.concatenate([ah, al], axis=dims[0][0]), jnp.concatenate([bl, bh], axis=0), dims
    )
    return first[:, :n] + (first[:, n:] + second[:, :n] + (second[:, n:] + small))


def eliminate(states, start, n):
    shape = (TILE, n)
    tiles = GROUP // TILE
    row = lax.broadcasted_iota(jnp.int32, shape, 0)

    def spread(value, i):
        return jnp.broadcast_to(value[i // TILE][i % TILE : i % TILE + 1, :], shape)

    halves = [
        [
            [state[pl.ds(pl.multiple_of(start + t * TILE, TILE), TILE), side] for t in range(tiles)]
            for side in (slice(0, n), slice(n, 2 * n))
        ]
        for state in states
    ]
    pivots = [[None] * tiles for _ in states]
    for first in range(0, GROUP, BLOCK):
        held = [
            {
                k: {
                    t: jnp.take_along_axis(
                        left[t], jnp.zeros(shape, jnp.int32) + (start + k), axis=1, mode="promise_in_bounds"
                    )
                    for t in range(k // TILE, tiles)
                }
                for k in range(first, first + BLOCK)
            }
            for left, _ in halves
        ]
        for i in range(first, first + BLOCK):
            at = i // TILE
            for cols, sides, pivot_of in zip(held, halves, pivots):
                pivot = spread(cols[i], i)
                pivot_of[at] = pivot if i % TILE == 0 else jnp.where(row == i % TILE, pivot, pivot_of[at])
                if i == GROUP - 1:
                    continue
                inverse = 1.0 / pivot
                below = dict(cols[i])
                below[at] = jnp.where(row > i % TILE, below[at], 0.0)
                factor = {t: below[t] * inverse for t in below}
                for k in range(i + 1, first + BLOCK):
                    across = spread(cols[i], k)
                    for t in cols[k]:
                        if k == i + 1:
                            cols[k][t] = cols[k][t] - (below[t] * across) * inverse
                        else:
                            cols[k][t] = cols[k][t] - factor[t] * across
                for side in sides:
                    across = spread(side, i)
                    for t in below:
                        side[t] = side[t] - factor[t] * across
    lane = lax.broadcasted_iota(jnp.int32, (GROUP, n), 1)
    rows = pl.ds(pl.multiple_of(start, GROUP), GROUP)
    for state, sides, pivot_of in zip(states, halves, pivots):
        scale = jnp.concatenate([lax.rsqrt(p) for p in pivot_of], axis=0)
        left, right = [jnp.concatenate(side, axis=0) * scale for side in sides]
        state[rows, :n] = left
        state[rows, n:] = right
        parts = split3(left)
        lhs = [jnp.where(lane >= start + GROUP, part, jnp.zeros_like(part)) for part in parts]
        rhs = [jnp.concatenate(pair, axis=1) for pair in zip(parts, split3(right))]
        state[...] = state[...] - deep_dot(lhs, rhs, TN)


def upper_blocks(size, n):
    count = size // n
    return [(i, j) for i in range(count) for j in range(i, count)]


def gram_kernel(divisor, n, place_ref, *refs):
    pieces, (columns_ref, gram_ref) = refs[:-2], refs[-2:]
    rows = pieces[0].shape[0]
    for distance, piece in enumerate(pieces):
        start = pl.multiple_of(lax.bitwise_xor(place_ref[0], distance) * rows, rows)
        columns_ref[pl.ds(start, rows), :] = piece[...]
    for b, (i, j) in enumerate(upper_blocks(columns_ref.shape[0], n)):
        product = dot(columns_ref[i * n : (i + 1) * n, :], columns_ref[j * n : (j + 1) * n, :], NT)
        gram_ref[b * n : (b + 1) * n, :] = product / divisor


def local_gram(place, pieces, divisor, n):
    rows, width = pieces[0].shape
    size = rows * len(pieces)
    vmem = pl.BlockSpec(memory_space=pltpu.VMEM)
    return pl.pallas_call(
        functools.partial(gram_kernel, divisor, n),
        out_shape=(
            jax.ShapeDtypeStruct((size, width), pieces[0].dtype),
            jax.ShapeDtypeStruct((len(upper_blocks(size, n)) * n, n), jnp.float32),
        ),
        in_specs=[pl.BlockSpec(memory_space=pltpu.SMEM)] + [vmem] * len(pieces),
        out_specs=(vmem, vmem),
        name="local_gram",
    )(place.reshape(1), *pieces)


def factor_kernel(blocks_ref, basis_ref, cols_ref, tri_ref, out_ref, core_ref, high, middle, lower, work, one, two):
    size = tri_ref.shape[0]
    n = basis_ref.shape[1]
    phases = size // n
    part = [slice(i * n, (i + 1) * n) for i in range(phases)]
    for b, (i, j) in enumerate(upper_blocks(size, n)):
        block = blocks_ref[b * n : (b + 1) * n, :]
        work[part[i], part[j]] = block
        for ref, piece in zip((high, middle, lower), split3(block)):
            ref[part[i], part[j]] = piece
            if i != j:
                ref[part[j], part[i]] = piece.T
        if i != j:
            tri_ref[part[i], part[j]] = jnp.zeros((n, n), jnp.float32)
    eye = (
        lax.broadcasted_iota(jnp.int32, (n, n), 0) == lax.broadcasted_iota(jnp.int32, (n, n), 1)
    ).astype(jnp.float32)
    upper = lax.broadcasted_iota(jnp.int32, (n, n), 0) <= lax.broadcasted_iota(jnp.int32, (n, n), 1)
    basis = basis_ref[...]
    for phase in range(max(phases, 2 * ITERS)):
        if phase < phases:
            at = part[phase]
            one[:, :n] = work[at, at]
            one[:, n:] = eye
        if phase < 2 * ITERS:
            if phase % 2 == 0:
                parts = split3(basis)
                wide = split3(wide_dot((high[...], middle[...], lower[...]), parts, NN))
                two[:, :n] = wide_dot(parts, wide, TN)
            else:
                wide = split3(wide)
                two[:, :n] = wide_dot(wide, wide, TN)
            two[:, n:] = eye

        def step(group, carry):
            states = [one] * (phase < phases) + [two] * (phase < 2 * ITERS)
            eliminate(states, group * GROUP, n)
            return carry

        lax.fori_loop(0, n // GROUP, step, 0)
        if phase < phases:
            tri_ref[at, at] = jnp.where(upper, one[:, :n], 0.0).T
            if phase < phases - 1:
                rest = slice((phase + 1) * n, size)
                panel = deep_dot(split3(one[:, n:]), split3(work[at, rest]), NN)
                tri_ref[rest, at] = panel.T
                pieces = split3(panel)
                for i in range(phase + 1, phases):
                    tail = slice((i - phase - 1) * n, None)
                    mine = slice((i - phase - 1) * n, (i - phase) * n)
                    work[part[i], i * n :] = work[part[i], i * n :] - deep_dot(
                        [x[:, mine] for x in pieces], [x[:, tail] for x in pieces], TN
                    )
        if phase < 2 * ITERS:
            wide = deep_dot(wide, split3(two[:, n:]), NT)
            if phase % 2 == 1:
                basis = wide
    out_ref[...] = basis
    core_ref[...] = dot(basis.astype(jnp.bfloat16), cols_ref[...], TN).astype(jnp.bfloat16)


def factor(blocks, basis, columns):
    size, n = basis.shape
    return pl.pallas_call(
        factor_kernel,
        out_shape=(
            jax.ShapeDtypeStruct((size, size), jnp.float32),
            jax.ShapeDtypeStruct((size, n), jnp.float32),
            jax.ShapeDtypeStruct((n, columns.shape[1]), jnp.bfloat16),
        ),
        scratch_shapes=[
            pltpu.VMEM((size, size), jnp.bfloat16),
            pltpu.VMEM((size, size), jnp.bfloat16),
            pltpu.VMEM((size, size), jnp.bfloat16),
            pltpu.VMEM((size, size), jnp.float32),
            pltpu.VMEM((n, 2 * n), jnp.float32),
            pltpu.VMEM((n, 2 * n), jnp.float32),
        ],
        compiler_params=pltpu.CompilerParams(vmem_limit_bytes=32 * 1024 * 1024),
        name="factor",
    )(blocks, basis, columns)


class Group:
    def __init__(self, bits):
        self.axes = tuple(dict.fromkeys(axis for axis, _ in bits))
        self.bits = bits
        self.size = 2 ** len(bits)
        self.me = 0
        for b, (axis, distance) in enumerate(bits):
            self.me = self.me + (((lax.axis_index(axis) // distance) % 2) << b)

    def swap(self, value, change):
        sizes = [lax.axis_size(axis) for axis in self.axes]
        pairs = []
        for source, place in enumerate(np.ndindex(*sizes)):
            place = list(place)
            for b, (axis, distance) in enumerate(self.bits):
                if (change >> b) & 1:
                    place[self.axes.index(axis)] ^= distance
            pairs.append((source, int(np.ravel_multi_index(place, sizes))))
        return lax.ppermute(value, self.axes, pairs)

    def scatter_sum(self, value):
        part = value.shape[0] // self.size
        got = [
            self.swap(lax.dynamic_slice_in_dim(value, (self.me ^ d) * part, part, 0), d)
            for d in range(1, self.size)
        ]
        return sum(got, lax.dynamic_slice_in_dim(value, self.me * part, part, 0))

    def gather(self, value):
        got = [value] + [self.swap(value, d) for d in range(1, self.size)]
        whole = jnp.zeros((self.size, *value.shape), value.dtype)
        for d in range(self.size):
            whole = lax.dynamic_update_slice_in_dim(whole, got[d][None], self.me ^ d, 0)
        return whole.reshape(self.size * value.shape[0], *value.shape[1:])


def axis_bits(axis):
    size = lax.axis_size(axis)
    assert size & (size - 1) == 0, axis
    return [(axis, 1 << b) for b in range(size.bit_length() - 1)]


def reduce_all(value):
    first, *rest = axis_bits("gy") + axis_bits("gz")
    groups = [Group([first])] + [Group(rest[b : b + 2]) for b in range(0, len(rest), 2)]
    for group in groups:
        value = group.scatter_sum(value)
    for bit in axis_bits("af"):
        value = value + Group([bit]).swap(value, 1)
    for group in reversed(groups):
        value = group.gather(value)
    return value


def on_device(slab, block_owner, basis_init):
    fibers = lax.axis_size("af")
    block_cols = slab.shape[1] // fibers
    owners = block_owner.reshape(fibers)
    labels = jnp.arange(fibers, dtype=jnp.int32)
    onehot = (owners[:, None] == labels[None, :]).astype(jnp.int32)
    source = jnp.sum(onehot * labels[:, None], axis=0)
    along = Group(axis_bits("af"))

    def block_of(distance):
        start = source[along.me ^ distance] * block_cols
        return lax.dynamic_slice_in_dim(slab, start, block_cols, 1)

    pieces = [block_of(0)]
    for distance in range(1, fibers):
        pieces.append(along.swap(block_of(distance), distance))
    devices_all = fibers * lax.axis_size("gy") * lax.axis_size("gz")
    columns, blocks = local_gram(along.me, pieces, block_cols * devices_all, basis_init.shape[1])
    return factor(reduce_all(blocks), basis_init, columns)


def solution(mesh):
    placed = (P("af", ("gy", "gz")), P("gy", "gz", None), P())
    return jax.shard_map(
        on_device,
        mesh=mesh,
        in_specs=placed,
        out_specs=(P(), P(), P(None, ("gy", "gz", "af"))),
        check_vma=False,
    )
```

```python
import functools

import jax
import jax.numpy as jnp
import numpy as np
from jax import lax
from jax.experimental import pallas as pl
from jax.experimental.pallas import tpu as pltpu
from jax.sharding import PartitionSpec as P

ITERS = 2
GROUP = 32
BLOCK = 16
TILE = 8


def split3(x):
    hi = x.astype(jnp.bfloat16)
    rest = x - hi.astype(jnp.float32)
    mid = rest.astype(jnp.bfloat16)
    low = (rest - mid.astype(jnp.float32)).astype(jnp.bfloat16)
    return hi, mid, low


def dot(a, b, dims):
    return lax.dot_general(a, b, (dims, ((), ())), preferred_element_type=jnp.float32)


NN, NT, TN = ((1,), (0,)), ((1,), (1,)), ((0,), (0,))


def deep_dot(a, b, dims):
    (ah, am, al), (bh, bm, bl) = a, b
    left = jnp.concatenate([ah, am, ah, am, ah, al], axis=dims[0][0])
    right = jnp.concatenate([bh, bh, bm, bm, bl, bh], axis=dims[1][0])
    return dot(left, right, dims)


def wide_dot(a, b, dims):
    (ah, am, al), (bh, bm, bl) = a, b
    n = bh.shape[1]
    both = jnp.concatenate([bh, bm], axis=1)
    first = dot(ah, both, dims)
    second = dot(am, both, dims)
    small = dot(
        jnp.concatenate([ah, al], axis=dims[0][0]), jnp.concatenate([bl, bh], axis=0), dims
    )
    return first[:, :n] + (first[:, n:] + second[:, :n] + (second[:, n:] + small))


def eliminate(states, start, n):
    shape = (TILE, n)
    tiles = GROUP // TILE
    row = lax.broadcasted_iota(jnp.int32, shape, 0)

    def spread(value, i):
        return jnp.broadcast_to(value[i // TILE][i % TILE : i % TILE + 1, :], shape)

    halves = [
        [
            [state[pl.ds(pl.multiple_of(start + t * TILE, TILE), TILE), side] for t in range(tiles)]
            for side in (slice(0, n), slice(n, 2 * n))
        ]
        for state in states
    ]
    pivots = [[None] * tiles for _ in states]
    for first in range(0, GROUP, BLOCK):
        held = [
            {
                k: {
                    t: jnp.take_along_axis(
                        left[t], jnp.zeros(shape, jnp.int32) + (start + k), axis=1, mode="promise_in_bounds"
                    )
                    for t in range(k // TILE, tiles)
                }
                for k in range(first, first + BLOCK)
            }
            for left, _ in halves
        ]
        for i in range(first, first + BLOCK):
            at = i // TILE
            for cols, sides, pivot_of in zip(held, halves, pivots):
                pivot = spread(cols[i], i)
                pivot_of[at] = pivot if i % TILE == 0 else jnp.where(row == i % TILE, pivot, pivot_of[at])
                if i == GROUP - 1:
                    continue
                inverse = 1.0 / pivot
                below = dict(cols[i])
                below[at] = jnp.where(row > i % TILE, below[at], 0.0)
                factor = {t: below[t] * inverse for t in below}
                for k in range(i + 1, first + BLOCK):
                    across = spread(cols[i], k)
                    for t in cols[k]:
                        if k == i + 1:
                            cols[k][t] = cols[k][t] - (below[t] * across) * inverse
                        else:
                            cols[k][t] = cols[k][t] - factor[t] * across
                for side in sides:
                    across = spread(side, i)
                    for t in below:
                        side[t] = side[t] - factor[t] * across
    lane = lax.broadcasted_iota(jnp.int32, (GROUP, n), 1)
    rows = pl.ds(pl.multiple_of(start, GROUP), GROUP)
    for state, sides, pivot_of in zip(states, halves, pivots):
        scale = jnp.concatenate([lax.rsqrt(p) for p in pivot_of], axis=0)
        left, right = [jnp.concatenate(side, axis=0) * scale for side in sides]
        state[rows, :n] = left
        state[rows, n:] = right
        parts = split3(left)
        lhs = [jnp.where(lane >= start + GROUP, part, jnp.zeros_like(part)) for part in parts]
        rhs = [jnp.concatenate(pair, axis=1) for pair in zip(parts, split3(right))]
        state[...] = state[...] - deep_dot(lhs, rhs, TN)


def upper_blocks(size, n):
    count = size // n
    return [(i, j) for i in range(count) for j in range(i, count)]


def axis_bits(axis):
    size = lax.axis_size(axis)
    assert size & (size - 1) == 0, axis
    return [(axis, 1 << b) for b in range(size.bit_length() - 1)]


def plane_groups():
    first, *rest = axis_bits("gy") + axis_bits("gz")
    return [[first]] + [rest[b : b + 2] for b in range(0, len(rest), 2)]


def place_in(bits):
    place = 0
    for axis, distance in bits:
        place = place * 2 + lax.bitwise_and(lax.axis_index(axis) // distance, 1)
    return place


def plane_place():
    return place_in(sum(plane_groups(), []))


def fiber_place():
    return lax.axis_index("af")


def pick_kernel(owner_ref, slab_ref, *refs):
    pieces, sems = refs[:-1], refs[-1]
    fibers = len(pieces)
    width = pieces[0].shape[1]
    me = fiber_place()
    copies = []
    for distance in range(fibers):
        block = 0
        for b in range(fibers):
            mine = owner_ref[0, 0, b] == lax.bitwise_xor(me, distance)
            block = jnp.where(mine, b, block)
        start = pl.multiple_of(block * width, width)
        copies.append(
            pltpu.make_async_copy(slab_ref.at[:, pl.ds(start, width)], pieces[distance], sems.at[distance])
        )
    for copy in copies:
        copy.start()
    for copy in copies:
        copy.wait()


def pick_blocks(owners, slab):
    fibers = owners.shape[-1]
    piece = jax.ShapeDtypeStruct((slab.shape[0], slab.shape[1] // fibers), slab.dtype)
    return pl.pallas_call(
        pick_kernel,
        out_shape=(piece,) * fibers,
        in_specs=[pl.BlockSpec(memory_space=pltpu.SMEM), pl.BlockSpec(memory_space=pl.ANY)],
        out_specs=(pl.BlockSpec(memory_space=pl.ANY),) * fibers,
        scratch_shapes=[pltpu.SemaphoreType.DMA((fibers,))],
        name="pick_blocks",
    )(owners, slab)


def in_row_order(pieces, columns):
    rows = pieces[0].shape[0]
    me = fiber_place()
    for distance, piece in enumerate(pieces):
        start = pl.multiple_of(lax.bitwise_xor(me, distance) * rows, rows)
        columns[pl.ds(start, rows), :] = piece[...]


def gram_kernel(divisor, n, chunks, *refs):
    pieces, (kept_ref, sent_ref, columns, blocks) = refs[:-4], refs[-4:]
    in_row_order(pieces, columns)
    for b, (i, j) in enumerate(upper_blocks(columns.shape[0], n)):
        product = dot(columns[i * n : (i + 1) * n, :], columns[j * n : (j + 1) * n, :], NT)
        blocks[b * n : (b + 1) * n, :] = product / divisor
    place = plane_place()
    rows = blocks.shape[0] // chunks
    for slot in range(chunks):
        start = pl.multiple_of(lax.bitwise_xor(place, slot) * rows, rows)
        target = kept_ref if slot < chunks // 2 else sent_ref
        at = slot % (chunks // 2) * rows
        target[at : at + rows, :] = blocks[pl.ds(start, rows), :]


def local_gram(pieces, divisor, n, chunks):
    rows, width = pieces[0].shape
    size = rows * len(pieces)
    total = len(upper_blocks(size, n)) * n
    half = jax.ShapeDtypeStruct((total // 2, n), jnp.float32)
    return pl.pallas_call(
        functools.partial(gram_kernel, divisor, n, chunks),
        out_shape=(half, half),
        scratch_shapes=[pltpu.VMEM((size, width), pieces[0].dtype), pltpu.VMEM((total, n), jnp.float32)],
        compiler_params=pltpu.CompilerParams(vmem_limit_bytes=32 * 1024 * 1024),
        name="local_gram",
    )(*pieces)


def factor_kernel(chunks, fibers, *refs):
    slots, refs = refs[: chunks // 2], refs[chunks // 2 :]
    other_ref, basis_ref, refs = refs[0], refs[1], refs[2:]
    pieces, refs = refs[:fibers], refs[fibers:]
    tri_ref, out_ref, core_ref, blocks_ref, columns, high, middle, lower, work, one, two = refs
    size = tri_ref.shape[0]
    n = basis_ref.shape[1]
    in_row_order(pieces, columns)
    place = plane_place()
    rows = slots[0].shape[0]
    for slot in range(chunks):
        start = pl.multiple_of(lax.bitwise_xor(place, slot) * rows, rows)
        at = slot % (chunks // 2)
        if slot < chunks // 2:
            blocks_ref[pl.ds(start, rows), :] = slots[at][...]
        else:
            blocks_ref[pl.ds(start, rows), :] = other_ref[at * rows : (at + 1) * rows, :]
    phases = size // n
    part = [slice(i * n, (i + 1) * n) for i in range(phases)]
    for b, (i, j) in enumerate(upper_blocks(size, n)):
        block = blocks_ref[b * n : (b + 1) * n, :]
        work[part[i], part[j]] = block
        for ref, piece in zip((high, middle, lower), split3(block)):
            ref[part[i], part[j]] = piece
            if i != j:
                ref[part[j], part[i]] = piece.T
        if i != j:
            tri_ref[part[i], part[j]] = jnp.zeros((n, n), jnp.float32)
    eye = (
        lax.broadcasted_iota(jnp.int32, (n, n), 0) == lax.broadcasted_iota(jnp.int32, (n, n), 1)
    ).astype(jnp.float32)
    upper = lax.broadcasted_iota(jnp.int32, (n, n), 0) <= lax.broadcasted_iota(jnp.int32, (n, n), 1)
    basis = basis_ref[...]
    for phase in range(max(phases, 2 * ITERS)):
        if phase < phases:
            at = part[phase]
            one[:, :n] = work[at, at]
            one[:, n:] = eye
        if phase < 2 * ITERS:
            if phase % 2 == 0:
                parts = split3(basis)
                wide = split3(wide_dot((high[...], middle[...], lower[...]), parts, NN))
                two[:, :n] = wide_dot(parts, wide, TN)
            else:
                wide = split3(wide)
                two[:, :n] = wide_dot(wide, wide, TN)
            two[:, n:] = eye

        def step(group, carry):
            states = [one] * (phase < phases) + [two] * (phase < 2 * ITERS)
            eliminate(states, group * GROUP, n)
            return carry

        lax.fori_loop(0, n // GROUP, step, 0)
        if phase < phases:
            tri_ref[at, at] = jnp.where(upper, one[:, :n], 0.0).T
            if phase < phases - 1:
                rest = slice((phase + 1) * n, size)
                panel = deep_dot(split3(one[:, n:]), split3(work[at, rest]), NN)
                tri_ref[rest, at] = panel.T
                pieces = split3(panel)
                for i in range(phase + 1, phases):
                    tail = slice((i - phase - 1) * n, None)
                    mine = slice((i - phase - 1) * n, (i - phase) * n)
                    work[part[i], i * n :] = work[part[i], i * n :] - deep_dot(
                        [x[:, mine] for x in pieces], [x[:, tail] for x in pieces], TN
                    )
        if phase < 2 * ITERS:
            wide = deep_dot(wide, split3(two[:, n:]), NT)
            if phase % 2 == 1:
                basis = wide
    out_ref[...] = basis
    core_ref[...] = dot(basis.astype(jnp.bfloat16), columns[...], TN).astype(jnp.bfloat16)


def factor(slots, other, basis, pieces):
    size, n = basis.shape
    width = pieces[0].shape[1]
    chunks = 2 * len(slots)
    return pl.pallas_call(
        functools.partial(factor_kernel, chunks, len(pieces)),
        out_shape=(
            jax.ShapeDtypeStruct((size, size), jnp.float32),
            jax.ShapeDtypeStruct((size, n), jnp.float32),
            jax.ShapeDtypeStruct((n, width), jnp.bfloat16),
        ),
        scratch_shapes=[
            pltpu.VMEM((2 * other.shape[0], n), jnp.float32),
            pltpu.VMEM((size, width), jnp.bfloat16),
            pltpu.VMEM((size, size), jnp.bfloat16),
            pltpu.VMEM((size, size), jnp.bfloat16),
            pltpu.VMEM((size, size), jnp.bfloat16),
            pltpu.VMEM((size, size), jnp.float32),
            pltpu.VMEM((n, 2 * n), jnp.float32),
            pltpu.VMEM((n, 2 * n), jnp.float32),
        ],
        compiler_params=pltpu.CompilerParams(vmem_limit_bytes=32 * 1024 * 1024),
        name="factor",
    )(*slots, other, basis, *pieces)


def swap(value, bits, change):
    axes = tuple(dict.fromkeys(axis for axis, _ in bits))
    sizes = [lax.axis_size(axis) for axis in axes]
    pairs = []
    for source, place in enumerate(np.ndindex(*sizes)):
        place = list(place)
        for b, (axis, distance) in enumerate(reversed(bits)):
            if (change >> b) & 1:
                place[axes.index(axis)] ^= distance
        pairs.append((source, int(np.ravel_multi_index(place, sizes))))
    return lax.ppermute(value, axes, pairs)


def sum_over_devices(kept, sent):
    first, *groups = plane_groups()
    value = kept + swap(sent, first, 1)
    for bits in groups:
        part = value.shape[0] >> len(bits)
        cuts = [value[d * part : (d + 1) * part] for d in range(1 << len(bits))]
        value = sum([swap(cuts[d], bits, d) for d in range(1, len(cuts))], cuts[0])
    for bit in axis_bits("af"):
        value = value + swap(value, [bit], 1)
    slots = [value]
    for bits in reversed(groups):
        whole = jnp.concatenate(slots, axis=0) if len(slots) > 1 else slots[0]
        slots = slots + [
            piece
            for d in range(1, 1 << len(bits))
            for piece in jnp.split(swap(whole, bits, d), len(slots), axis=0)
        ]
    return slots, swap(jnp.concatenate(slots, axis=0), first, 1)


def on_device(slab, block_owner, basis_init):
    fibers = lax.axis_size("af")
    chunks = lax.axis_size("gy") * lax.axis_size("gz")
    along = axis_bits("af")
    pieces = pick_blocks(block_owner, slab)
    pieces = [pieces[0]] + [swap(pieces[d], along[::-1], d) for d in range(1, fibers)]
    divisor = pieces[0].shape[1] * fibers * chunks
    kept, sent = local_gram(pieces, divisor, basis_init.shape[1], chunks)
    slots, other = sum_over_devices(kept, sent)
    return factor(slots, other, basis_init, pieces)


def solution(mesh):
    placed = (P("af", ("gy", "gz")), P("gy", "gz", None), P())
    return jax.shard_map(
        on_device,
        mesh=mesh,
        in_specs=placed,
        out_specs=(P(), P(), P(None, ("gy", "gz", "af"))),
        check_vma=False,
    )
```

```python
import functools

import jax
import jax.numpy as jnp
import numpy as np
from jax import lax
from jax.experimental import pallas as pl
from jax.experimental.pallas import tpu as pltpu
from jax.sharding import PartitionSpec as P

ITERS = 2
GROUP = 32
BLOCK = 16
TILE = 8


def split3(x):
    hi = x.astype(jnp.bfloat16)
    rest = x - hi.astype(jnp.float32)
    mid = rest.astype(jnp.bfloat16)
    low = (rest - mid.astype(jnp.float32)).astype(jnp.bfloat16)
    return hi, mid, low


def dot(a, b, dims):
    return lax.dot_general(a, b, (dims, ((), ())), preferred_element_type=jnp.float32)


NN, NT, TN = ((1,), (0,)), ((1,), (1,)), ((0,), (0,))


def deep_dot(a, b, dims):
    (ah, am, al), (bh, bm, bl) = a, b
    left = jnp.concatenate([ah, am, ah, am, ah, al], axis=dims[0][0])
    right = jnp.concatenate([bh, bh, bm, bm, bl, bh], axis=dims[1][0])
    return dot(left, right, dims)


def wide_dot(a, b, dims):
    (ah, am, al), (bh, bm, bl) = a, b
    n = bh.shape[1]
    both = jnp.concatenate([bh, bm], axis=1)
    first = dot(ah, both, dims)
    second = dot(am, both, dims)
    small = dot(
        jnp.concatenate([ah, al], axis=dims[0][0]), jnp.concatenate([bl, bh], axis=0), dims
    )
    return first[:, :n] + (first[:, n:] + second[:, :n] + (second[:, n:] + small))


def eliminate(states, start, n):
    shape = (TILE, n)
    tiles = GROUP // TILE
    row = lax.broadcasted_iota(jnp.int32, shape, 0)

    def spread(value, i):
        return jnp.broadcast_to(value[i // TILE][i % TILE : i % TILE + 1, :], shape)

    halves = [
        [
            [state[pl.ds(pl.multiple_of(start + t * TILE, TILE), TILE), side] for t in range(tiles)]
            for side in (slice(0, n), slice(n, 2 * n))
        ]
        for state in states
    ]
    pivots = [[None] * tiles for _ in states]
    for first in range(0, GROUP, BLOCK):
        held = [
            {
                k: {
                    t: jnp.take_along_axis(
                        left[t], jnp.zeros(shape, jnp.int32) + (start + k), axis=1, mode="promise_in_bounds"
                    )
                    for t in range(k // TILE, tiles)
                }
                for k in range(first, first + BLOCK)
            }
            for left, _ in halves
        ]
        for i in range(first, first + BLOCK):
            at = i // TILE
            for cols, sides, pivot_of in zip(held, halves, pivots):
                pivot = spread(cols[i], i)
                pivot_of[at] = pivot if i % TILE == 0 else jnp.where(row == i % TILE, pivot, pivot_of[at])
                if i == GROUP - 1:
                    continue
                inverse = 1.0 / pivot
                below = dict(cols[i])
                below[at] = jnp.where(row > i % TILE, below[at], 0.0)
                factor = {t: below[t] * inverse for t in below}
                for k in range(i + 1, first + BLOCK):
                    across = spread(cols[i], k)
                    for t in cols[k]:
                        if k == i + 1:
                            cols[k][t] = cols[k][t] - (below[t] * across) * inverse
                        else:
                            cols[k][t] = cols[k][t] - factor[t] * across
                for side in sides:
                    across = spread(side, i)
                    for t in below:
                        side[t] = side[t] - factor[t] * across
    lane = lax.broadcasted_iota(jnp.int32, (GROUP, n), 1)
    rows = pl.ds(pl.multiple_of(start, GROUP), GROUP)
    for state, sides, pivot_of in zip(states, halves, pivots):
        scale = jnp.concatenate([lax.rsqrt(p) for p in pivot_of], axis=0)
        left, right = [jnp.concatenate(side, axis=0) * scale for side in sides]
        state[rows, :n] = left
        state[rows, n:] = right
        parts = split3(left)
        lhs = [jnp.where(lane >= start + GROUP, part, jnp.zeros_like(part)) for part in parts]
        rhs = [jnp.concatenate(pair, axis=1) for pair in zip(parts, split3(right))]
        state[...] = state[...] - deep_dot(lhs, rhs, TN)


def upper_blocks(size, n):
    count = size // n
    return [(i, j) for i in range(count) for j in range(i, count)]


def axis_bits(axis):
    size = lax.axis_size(axis)
    assert size & (size - 1) == 0, axis
    return [(axis, 1 << b) for b in range(size.bit_length() - 1)]


def plane_groups():
    first, *rest = axis_bits("gy") + axis_bits("gz")
    return [[first]] + [rest[b : b + 2] for b in range(0, len(rest), 2)]


def place_in(bits):
    place = 0
    for axis, distance in bits:
        place = place * 2 + lax.bitwise_and(lax.axis_index(axis) // distance, 1)
    return place


def plane_place():
    return place_in(sum(plane_groups(), []))


def fiber_place():
    return lax.axis_index("af")


def pick_kernel(owner_ref, slab_ref, *pieces):
    fibers = len(pieces)
    width = pieces[0].shape[1]
    me = fiber_place()
    for distance, piece in enumerate(pieces):
        block = 0
        for b in range(fibers):
            block = jnp.where(owner_ref[0, 0, b] == lax.bitwise_xor(me, distance), b, block)
        piece[...] = slab_ref[:, pl.ds(pl.multiple_of(block * width, width), width)]


def pick_blocks(owners, slab):
    fibers = owners.shape[-1]
    piece = jax.ShapeDtypeStruct((slab.shape[0], slab.shape[1] // fibers), slab.dtype)
    return pl.pallas_call(
        pick_kernel,
        out_shape=(piece,) * fibers,
        in_specs=[pl.BlockSpec(memory_space=pltpu.SMEM), pl.BlockSpec(memory_space=pltpu.VMEM)],
        name="pick_blocks",
    )(owners, slab)


def in_row_order(pieces, columns):
    rows = pieces[0].shape[0]
    me = fiber_place()
    for distance, piece in enumerate(pieces):
        start = pl.multiple_of(lax.bitwise_xor(me, distance) * rows, rows)
        columns[pl.ds(start, rows), :] = piece[...]


def gram_kernel(divisor, n, chunks, *refs):
    pieces, (kept_ref, sent_ref, columns, blocks) = refs[:-4], refs[-4:]
    in_row_order(pieces, columns)
    for b, (i, j) in enumerate(upper_blocks(columns.shape[0], n)):
        product = dot(columns[i * n : (i + 1) * n, :], columns[j * n : (j + 1) * n, :], NT)
        blocks[b * n : (b + 1) * n, :] = product / divisor
    place = plane_place()
    rows = blocks.shape[0] // chunks
    for slot in range(chunks):
        start = pl.multiple_of(lax.bitwise_xor(place, slot) * rows, rows)
        target = kept_ref if slot < chunks // 2 else sent_ref
        at = slot % (chunks // 2) * rows
        target[at : at + rows, :] = blocks[pl.ds(start, rows), :]


def local_gram(pieces, divisor, n, chunks):
    rows, width = pieces[0].shape
    size = rows * len(pieces)
    total = len(upper_blocks(size, n)) * n
    half = jax.ShapeDtypeStruct((total // 2, n), jnp.float32)
    return pl.pallas_call(
        functools.partial(gram_kernel, divisor, n, chunks),
        out_shape=(half, half),
        scratch_shapes=[pltpu.VMEM((size, width), pieces[0].dtype), pltpu.VMEM((total, n), jnp.float32)],
        compiler_params=pltpu.CompilerParams(vmem_limit_bytes=32 * 1024 * 1024),
        name="local_gram",
    )(*pieces)


def factor_kernel(chunks, fibers, *refs):
    slots, refs = refs[: chunks // 2], refs[chunks // 2 :]
    other_ref, basis_ref, refs = refs[0], refs[1], refs[2:]
    pieces, refs = refs[:fibers], refs[fibers:]
    tri_ref, out_ref, core_ref, blocks_ref, columns, high, middle, lower, work, one, two = refs
    size = tri_ref.shape[0]
    n = basis_ref.shape[1]
    in_row_order(pieces, columns)
    place = plane_place()
    rows = slots[0].shape[0]
    for slot in range(chunks):
        start = pl.multiple_of(lax.bitwise_xor(place, slot) * rows, rows)
        at = slot % (chunks // 2)
        if slot < chunks // 2:
            blocks_ref[pl.ds(start, rows), :] = slots[at][...]
        else:
            blocks_ref[pl.ds(start, rows), :] = other_ref[at * rows : (at + 1) * rows, :]
    phases = size // n
    part = [slice(i * n, (i + 1) * n) for i in range(phases)]
    for b, (i, j) in enumerate(upper_blocks(size, n)):
        block = blocks_ref[b * n : (b + 1) * n, :]
        work[part[i], part[j]] = block
        for ref, piece in zip((high, middle, lower), split3(block)):
            ref[part[i], part[j]] = piece
            if i != j:
                ref[part[j], part[i]] = piece.T
        if i != j:
            tri_ref[part[i], part[j]] = jnp.zeros((n, n), jnp.float32)
    eye = (
        lax.broadcasted_iota(jnp.int32, (n, n), 0) == lax.broadcasted_iota(jnp.int32, (n, n), 1)
    ).astype(jnp.float32)
    upper = lax.broadcasted_iota(jnp.int32, (n, n), 0) <= lax.broadcasted_iota(jnp.int32, (n, n), 1)
    basis = basis_ref[...]
    for phase in range(max(phases, 2 * ITERS)):
        if phase < phases:
            at = part[phase]
            one[:, :n] = work[at, at]
            one[:, n:] = eye
        if phase < 2 * ITERS:
            if phase % 2 == 0:
                parts = split3(basis)
                wide = split3(wide_dot((high[...], middle[...], lower[...]), parts, NN))
                two[:, :n] = wide_dot(parts, wide, TN)
            else:
                wide = split3(wide)
                two[:, :n] = wide_dot(wide, wide, TN)
            two[:, n:] = eye

        def step(group, carry):
            states = [one] * (phase < phases) + [two] * (phase < 2 * ITERS)
            eliminate(states, group * GROUP, n)
            return carry

        lax.fori_loop(0, n // GROUP, step, 0)
        if phase < phases:
            tri_ref[at, at] = jnp.where(upper, one[:, :n], 0.0).T
            if phase < phases - 1:
                rest = slice((phase + 1) * n, size)
                panel = deep_dot(split3(one[:, n:]), split3(work[at, rest]), NN)
                tri_ref[rest, at] = panel.T
                pieces = split3(panel)
                for i in range(phase + 1, phases):
                    tail = slice((i - phase - 1) * n, None)
                    mine = slice((i - phase - 1) * n, (i - phase) * n)
                    work[part[i], i * n :] = work[part[i], i * n :] - deep_dot(
                        [x[:, mine] for x in pieces], [x[:, tail] for x in pieces], TN
                    )
        if phase < 2 * ITERS:
            wide = deep_dot(wide, split3(two[:, n:]), NT)
            if phase % 2 == 1:
                basis = wide
    out_ref[...] = basis
    core_ref[...] = dot(basis.astype(jnp.bfloat16), columns[...], TN).astype(jnp.bfloat16)


def factor(slots, other, basis, pieces):
    size, n = basis.shape
    width = pieces[0].shape[1]
    chunks = 2 * len(slots)
    return pl.pallas_call(
        functools.partial(factor_kernel, chunks, len(pieces)),
        out_shape=(
            jax.ShapeDtypeStruct((size, size), jnp.float32),
            jax.ShapeDtypeStruct((size, n), jnp.float32),
            jax.ShapeDtypeStruct((n, width), jnp.bfloat16),
        ),
        scratch_shapes=[
            pltpu.VMEM((2 * other.shape[0], n), jnp.float32),
            pltpu.VMEM((size, width), jnp.bfloat16),
            pltpu.VMEM((size, size), jnp.bfloat16),
            pltpu.VMEM((size, size), jnp.bfloat16),
            pltpu.VMEM((size, size), jnp.bfloat16),
            pltpu.VMEM((size, size), jnp.float32),
            pltpu.VMEM((n, 2 * n), jnp.float32),
            pltpu.VMEM((n, 2 * n), jnp.float32),
        ],
        compiler_params=pltpu.CompilerParams(vmem_limit_bytes=32 * 1024 * 1024),
        name="factor",
    )(*slots, other, basis, *pieces)


def swap(value, bits, change):
    axes = tuple(dict.fromkeys(axis for axis, _ in bits))
    sizes = [lax.axis_size(axis) for axis in axes]
    pairs = []
    for source, place in enumerate(np.ndindex(*sizes)):
        place = list(place)
        for b, (axis, distance) in enumerate(reversed(bits)):
            if (change >> b) & 1:
                place[axes.index(axis)] ^= distance
        pairs.append((source, int(np.ravel_multi_index(place, sizes))))
    return lax.ppermute(value, axes, pairs)


def sum_over_devices(kept, sent):
    first, *groups = plane_groups()
    value = kept + swap(sent, first, 1)
    for bits in groups:
        part = value.shape[0] >> len(bits)
        cuts = [value[d * part : (d + 1) * part] for d in range(1 << len(bits))]
        value = sum([swap(cuts[d], bits, d) for d in range(1, len(cuts))], cuts[0])
    for bit in axis_bits("af"):
        value = value + swap(value, [bit], 1)
    slots = [value]
    for bits in reversed(groups):
        whole = jnp.concatenate(slots, axis=0) if len(slots) > 1 else slots[0]
        slots = slots + [
            piece
            for d in range(1, 1 << len(bits))
            for piece in jnp.split(swap(whole, bits, d), len(slots), axis=0)
        ]
    return slots, swap(jnp.concatenate(slots, axis=0), first, 1)


def on_device(slab, block_owner, basis_init):
    fibers = lax.axis_size("af")
    chunks = lax.axis_size("gy") * lax.axis_size("gz")
    along = axis_bits("af")
    pieces = pick_blocks(block_owner, slab)
    pieces = [pieces[0]] + [swap(pieces[d], along[::-1], d) for d in range(1, fibers)]
    divisor = pieces[0].shape[1] * fibers * chunks
    kept, sent = local_gram(pieces, divisor, basis_init.shape[1], chunks)
    slots, other = sum_over_devices(kept, sent)
    return factor(slots, other, basis_init, pieces)


def solution(mesh):
    placed = (P("af", ("gy", "gz")), P("gy", "gz", None), P())
    return jax.shard_map(
        on_device,
        mesh=mesh,
        in_specs=placed,
        out_specs=(P(), P(), P(None, ("gy", "gz", "af"))),
        check_vma=False,
    )
```

```python
import functools

import jax
import jax.numpy as jnp
import numpy as np
from jax import lax
from jax.experimental import pallas as pl
from jax.experimental.pallas import tpu as pltpu
from jax.sharding import PartitionSpec as P

ITERS = 2
GROUP = 32
BLOCK = 16
TILE = 8


def split3(x):
    hi = x.astype(jnp.bfloat16)
    rest = x - hi.astype(jnp.float32)
    mid = rest.astype(jnp.bfloat16)
    low = (rest - mid.astype(jnp.float32)).astype(jnp.bfloat16)
    return hi, mid, low


def dot(a, b, dims):
    return lax.dot_general(a, b, (dims, ((), ())), preferred_element_type=jnp.float32)


NN, NT, TN = ((1,), (0,)), ((1,), (1,)), ((0,), (0,))


def deep_dot(a, b, dims):
    (ah, am, al), (bh, bm, bl) = a, b
    left = jnp.concatenate([ah, am, ah, am, ah, al], axis=dims[0][0])
    right = jnp.concatenate([bh, bh, bm, bm, bl, bh], axis=dims[1][0])
    return dot(left, right, dims)


def wide_dot(a, b, dims):
    (ah, am, al), (bh, bm, bl) = a, b
    n = bh.shape[1]
    both = jnp.concatenate([bh, bm], axis=1)
    first = dot(ah, both, dims)
    second = dot(am, both, dims)
    small = dot(
        jnp.concatenate([ah, al], axis=dims[0][0]), jnp.concatenate([bl, bh], axis=0), dims
    )
    return first[:, :n] + (first[:, n:] + second[:, :n] + (second[:, n:] + small))


def eliminate(states, start, n):
    shape = (TILE, n)
    tiles = GROUP // TILE
    row = lax.broadcasted_iota(jnp.int32, shape, 0)

    def spread(value, i):
        return jnp.broadcast_to(value[i // TILE][i % TILE : i % TILE + 1, :], shape)

    halves = [
        [
            [state[start + t * TILE : start + (t + 1) * TILE, side] for t in range(tiles)]
            for side in (slice(0, n), slice(n, 2 * n))
        ]
        for state in states
    ]
    pivots = [[None] * tiles for _ in states]
    for first in range(0, GROUP, BLOCK):
        held = [
            {
                k: {
                    t: jnp.take_along_axis(left[t], jnp.full(shape, start + k, jnp.int32), axis=1, mode="promise_in_bounds")
                    for t in range(k // TILE, tiles)
                }
                for k in range(first, first + BLOCK)
            }
            for left, _ in halves
        ]
        for i in range(first, first + BLOCK):
            at = i // TILE
            for cols, sides, pivot_of in zip(held, halves, pivots):
                pivot = spread(cols[i], i)
                pivot_of[at] = pivot if i % TILE == 0 else jnp.where(row == i % TILE, pivot, pivot_of[at])
                if i == GROUP - 1:
                    continue
                inverse = 1.0 / pivot
                below = dict(cols[i])
                below[at] = jnp.where(row > i % TILE, below[at], 0.0)
                factor = {t: below[t] * inverse for t in below}
                for k in range(i + 1, first + BLOCK):
                    across = spread(cols[i], k)
                    for t in cols[k]:
                        if k == i + 1:
                            cols[k][t] = cols[k][t] - (below[t] * across) * inverse
                        else:
                            cols[k][t] = cols[k][t] - factor[t] * across
                for side in sides:
                    across = spread(side, i)
                    for t in below:
                        side[t] = side[t] - factor[t] * across
    rows = slice(start, start + GROUP)
    rest = slice(start + GROUP, n)
    for state, sides, pivot_of in zip(states, halves, pivots):
        scale = jnp.concatenate([lax.rsqrt(p) for p in pivot_of], axis=0)
        left, right = [jnp.concatenate(side, axis=0) * scale for side in sides]
        state[rows, :n] = left
        state[rows, n:] = right
        if start + GROUP < n:
            lhs = split3(left)
            rhs = [jnp.concatenate(pair, axis=1) for pair in zip(lhs, split3(right))]
            state[rest, :] = state[rest, :] - deep_dot(lhs, rhs, TN)[rest, :]


def upper_blocks(size, n):
    count = size // n
    return [(i, j) for i in range(count) for j in range(i, count)]


def axis_bits(axis):
    size = lax.axis_size(axis)
    assert size & (size - 1) == 0, axis
    return [(axis, 1 << b) for b in range(size.bit_length() - 1)]


def plane_groups():
    first, *rest = axis_bits("gy") + axis_bits("gz")
    return [[first]] + [rest[b : b + 2] for b in range(0, len(rest), 2)]


def place_in(bits):
    place = 0
    for axis, distance in bits:
        place = place * 2 + lax.bitwise_and(lax.axis_index(axis) // distance, 1)
    return place


def plane_place():
    return place_in(sum(plane_groups(), []))


def fiber_place():
    return lax.axis_index("af")


def pick_kernel(distances, owner_ref, slab_ref, *pieces):
    width = pieces[0].shape[1]
    me = fiber_place()
    for distance, piece in zip(distances, pieces):
        block = 0
        for b in range(owner_ref.shape[-1]):
            block = jnp.where(owner_ref[0, 0, b] == lax.bitwise_xor(me, distance), b, block)
        piece[...] = slab_ref[:, pl.ds(pl.multiple_of(block * width, width), width)]


def pick_blocks(distances, owners, slab, **params):
    piece = jax.ShapeDtypeStruct((slab.shape[0], slab.shape[1] // owners.shape[-1]), slab.dtype)
    picked = pl.pallas_call(
        functools.partial(pick_kernel, distances),
        out_shape=(piece,) * len(distances),
        in_specs=[pl.BlockSpec(memory_space=pltpu.SMEM), pl.BlockSpec(memory_space=pltpu.VMEM)],
        compiler_params=pltpu.CompilerParams(**params),
        name="pick_blocks",
    )(owners, slab)
    return dict(zip(distances, picked))


def in_row_order(pieces, columns):
    rows = pieces[0].shape[0]
    me = fiber_place()
    for distance, piece in enumerate(pieces):
        start = pl.multiple_of(lax.bitwise_xor(me, distance) * rows, rows)
        columns[pl.ds(start, rows), :] = piece[...]


def gram_kernel(divisor, n, chunks, *refs):
    pieces, (kept_ref, sent_ref, columns, blocks) = refs[:-4], refs[-4:]
    in_row_order(pieces, columns)
    for b, (i, j) in enumerate(upper_blocks(columns.shape[0], n)):
        product = dot(columns[i * n : (i + 1) * n, :], columns[j * n : (j + 1) * n, :], NT)
        blocks[b * n : (b + 1) * n, :] = product / divisor
    place = plane_place()
    rows = blocks.shape[0] // chunks
    for slot in range(chunks):
        start = pl.multiple_of(lax.bitwise_xor(place, slot) * rows, rows)
        target = kept_ref if slot < chunks // 2 else sent_ref
        at = slot % (chunks // 2) * rows
        target[at : at + rows, :] = blocks[pl.ds(start, rows), :]


def local_gram(pieces, divisor, n, chunks):
    rows, width = pieces[0].shape
    size = rows * len(pieces)
    total = len(upper_blocks(size, n)) * n
    half = jax.ShapeDtypeStruct((total // 2, n), jnp.float32)
    return pl.pallas_call(
        functools.partial(gram_kernel, divisor, n, chunks),
        out_shape=(half, half),
        scratch_shapes=[pltpu.VMEM((size, width), pieces[0].dtype), pltpu.VMEM((total, n), jnp.float32)],
        compiler_params=pltpu.CompilerParams(vmem_limit_bytes=32 * 1024 * 1024),
        name="local_gram",
    )(*pieces)


def factor_kernel(chunks, fibers, *refs):
    slots, refs = refs[: chunks // 2], refs[chunks // 2 :]
    other_ref, basis_ref, refs = refs[0], refs[1], refs[2:]
    pieces, refs = refs[:fibers], refs[fibers:]
    tri_ref, out_ref, core_ref, blocks_ref, columns, high, middle, lower, work, one, two = refs
    size = tri_ref.shape[0]
    n = basis_ref.shape[1]
    in_row_order(pieces, columns)
    place = plane_place()
    rows = slots[0].shape[0]
    for slot in range(chunks):
        start = pl.multiple_of(lax.bitwise_xor(place, slot) * rows, rows)
        at = slot % (chunks // 2)
        if slot < chunks // 2:
            blocks_ref[pl.ds(start, rows), :] = slots[at][...]
        else:
            blocks_ref[pl.ds(start, rows), :] = other_ref[at * rows : (at + 1) * rows, :]
    phases = size // n
    part = [slice(i * n, (i + 1) * n) for i in range(phases)]
    for b, (i, j) in enumerate(upper_blocks(size, n)):
        block = blocks_ref[b * n : (b + 1) * n, :]
        work[part[i], part[j]] = block
        for ref, piece in zip((high, middle, lower), split3(block)):
            ref[part[i], part[j]] = piece
            if i != j:
                ref[part[j], part[i]] = piece.T
        if i != j:
            tri_ref[part[i], part[j]] = jnp.zeros((n, n), jnp.float32)
    eye = (
        lax.broadcasted_iota(jnp.int32, (n, n), 0) == lax.broadcasted_iota(jnp.int32, (n, n), 1)
    ).astype(jnp.float32)
    upper = lax.broadcasted_iota(jnp.int32, (n, n), 0) <= lax.broadcasted_iota(jnp.int32, (n, n), 1)
    basis = basis_ref[...]
    for phase in range(max(phases, 2 * ITERS)):
        if phase < phases:
            at = part[phase]
            one[:, :n] = work[at, at]
            one[:, n:] = eye
        if phase < 2 * ITERS:
            if phase % 2 == 0:
                parts = split3(basis)
                wide = split3(wide_dot((high[...], middle[...], lower[...]), parts, NN))
                two[:, :n] = wide_dot(parts, wide, TN)
            else:
                wide = split3(wide)
                two[:, :n] = wide_dot(wide, wide, TN)
            two[:, n:] = eye

        states = [one] * (phase < phases) + [two] * (phase < 2 * ITERS)
        for group in range(n // GROUP):
            eliminate(states, group * GROUP, n)
        if phase < phases:
            tri_ref[at, at] = jnp.where(upper, one[:, :n], 0.0).T
            if phase < phases - 1:
                rest = slice((phase + 1) * n, size)
                panel = deep_dot(split3(one[:, n:]), split3(work[at, rest]), NN)
                tri_ref[rest, at] = panel.T
                pieces = split3(panel)
                for i in range(phase + 1, phases):
                    tail = slice((i - phase - 1) * n, None)
                    mine = slice((i - phase - 1) * n, (i - phase) * n)
                    work[part[i], i * n :] = work[part[i], i * n :] - deep_dot(
                        [x[:, mine] for x in pieces], [x[:, tail] for x in pieces], TN
                    )
        if phase < 2 * ITERS:
            wide = deep_dot(wide, split3(two[:, n:]), NT)
            if phase % 2 == 1:
                basis = wide
    out_ref[...] = basis
    core_ref[...] = dot(basis.astype(jnp.bfloat16), columns[...], TN).astype(jnp.bfloat16)


def factor(slots, other, basis, pieces):
    size, n = basis.shape
    width = pieces[0].shape[1]
    chunks = 2 * len(slots)
    return pl.pallas_call(
        functools.partial(factor_kernel, chunks, len(pieces)),
        out_shape=(
            jax.ShapeDtypeStruct((size, size), jnp.float32),
            jax.ShapeDtypeStruct((size, n), jnp.float32),
            jax.ShapeDtypeStruct((n, width), jnp.bfloat16),
        ),
        scratch_shapes=[
            pltpu.VMEM((2 * other.shape[0], n), jnp.float32),
            pltpu.VMEM((size, width), jnp.bfloat16),
            pltpu.VMEM((size, size), jnp.bfloat16),
            pltpu.VMEM((size, size), jnp.bfloat16),
            pltpu.VMEM((size, size), jnp.bfloat16),
            pltpu.VMEM((size, size), jnp.float32),
            pltpu.VMEM((n, 2 * n), jnp.float32),
            pltpu.VMEM((n, 2 * n), jnp.float32),
        ],
        compiler_params=pltpu.CompilerParams(vmem_limit_bytes=32 * 1024 * 1024),
        name="factor",
    )(*slots, other, basis, *pieces)


def swap(value, bits, change):
    axes = tuple(dict.fromkeys(axis for axis, _ in bits))
    sizes = [lax.axis_size(axis) for axis in axes]
    pairs = []
    for source, place in enumerate(np.ndindex(*sizes)):
        place = list(place)
        for b, (axis, distance) in enumerate(reversed(bits)):
            if (change >> b) & 1:
                place[axes.index(axis)] ^= distance
        pairs.append((source, int(np.ravel_multi_index(place, sizes))))
    return lax.ppermute(value, axes, pairs)


def sum_over_devices(kept, sent):
    first, *groups = plane_groups()
    value = kept + swap(sent, first, 1)
    for bits in groups:
        part = value.shape[0] >> len(bits)
        cuts = [value[d * part : (d + 1) * part] for d in range(1 << len(bits))]
        value = sum([swap(cuts[d], bits, d) for d in range(1, len(cuts))], cuts[0])
    for bit in axis_bits("af"):
        value = value + swap(value, [bit], 1)
    slots = [value]
    for bits in reversed(groups):
        whole = jnp.concatenate(slots, axis=0) if len(slots) > 1 else slots[0]
        slots = slots + [
            piece
            for d in range(1, 1 << len(bits))
            for piece in jnp.split(swap(whole, bits, d), len(slots), axis=0)
        ]
    return slots, swap(jnp.concatenate(slots, axis=0), first, 1)


def on_device(slab, block_owner, basis_init):
    fibers = lax.axis_size("af")
    chunks = lax.axis_size("gy") * lax.axis_size("gz")
    along = axis_bits("af")[::-1]
    far = fibers // 2
    pieces = pick_blocks([far], block_owner, slab)
    slab, _ = lax.optimization_barrier((slab, pieces[far]))
    others = [d for d in range(fibers) if d != far]
    pieces.update(pick_blocks(others, block_owner, slab, vmem_limit_bytes=8 * 1024 * 1024))
    pieces = [pieces[0]] + [swap(pieces[d], along, d) for d in range(1, fibers)]
    divisor = pieces[0].shape[1] * fibers * chunks
    kept, sent = local_gram(pieces, divisor, basis_init.shape[1], chunks)
    slots, other = sum_over_devices(kept, sent)
    return factor(slots, other, basis_init, pieces)


def solution(mesh):
    placed = (P("af", ("gy", "gz")), P("gy", "gz", None), P())
    return jax.shard_map(
        on_device,
        mesh=mesh,
        in_specs=placed,
        out_specs=(P(), P(), P(None, ("gy", "gz", "af"))),
        check_vma=False,
    )
```

```python
import functools

import jax
import jax.numpy as jnp
import numpy as np
from jax import lax
from jax.experimental import pallas as pl
from jax.experimental.pallas import tpu as pltpu
from jax.sharding import PartitionSpec as P

ITERS = 2
GROUP = 32
BLOCK = 16
TILE = 8


def split3(x):
    hi = x.astype(jnp.bfloat16)
    rest = x - hi.astype(jnp.float32)
    mid = rest.astype(jnp.bfloat16)
    low = (rest - mid.astype(jnp.float32)).astype(jnp.bfloat16)
    return hi, mid, low


def dot(a, b, dims):
    return lax.dot_general(a, b, (dims, ((), ())), preferred_element_type=jnp.float32)


NN, NT, TN = ((1,), (0,)), ((1,), (1,)), ((0,), (0,))


def deep_dot(a, b, dims):
    (ah, am, al), (bh, bm, bl) = a, b
    left = jnp.concatenate([ah, am, ah, am, ah, al], axis=dims[0][0])
    right = jnp.concatenate([bh, bh, bm, bm, bl, bh], axis=dims[1][0])
    return dot(left, right, dims)


def short_dot(a, b, dims):
    (ah, am, _), (bh, bm, _) = a, b
    left = jnp.concatenate([ah, am, ah], axis=dims[0][0])
    right = jnp.concatenate([bh, bh, bm], axis=dims[1][0])
    return dot(left, right, dims)


def wide_dot(a, b, dims):
    (ah, am, al), (bh, bm, bl) = a, b
    n = bh.shape[1]
    both = jnp.concatenate([bh, bm], axis=1)
    first = dot(ah, both, dims)
    second = dot(am, both, dims)
    small = dot(
        jnp.concatenate([ah, al], axis=dims[0][0]), jnp.concatenate([bl, bh], axis=0), dims
    )
    return first[:, :n] + (first[:, n:] + second[:, :n] + (second[:, n:] + small))


def eliminate(states, start, n):
    shape = (TILE, n)
    tiles = GROUP // TILE
    row = lax.broadcasted_iota(jnp.int32, shape, 0)

    def spread(value, i):
        return jnp.broadcast_to(value[i // TILE][i % TILE : i % TILE + 1, :], shape)

    halves = [
        [
            [state[start + t * TILE : start + (t + 1) * TILE, side] for t in range(tiles)]
            for side in (slice(0, n), slice(n, 2 * n))
        ]
        for state in states
    ]
    pivots = [[None] * tiles for _ in states]
    for first in range(0, GROUP, BLOCK):
        held = [
            {
                k: {
                    t: jnp.take_along_axis(left[t], jnp.full(shape, start + k, jnp.int32), axis=1, mode="promise_in_bounds")
                    for t in range(k // TILE, tiles)
                }
                for k in range(first, first + BLOCK)
            }
            for left, _ in halves
        ]
        for i in range(first, first + BLOCK):
            at = i // TILE
            for cols, sides, pivot_of in zip(held, halves, pivots):
                pivot = spread(cols[i], i)
                pivot_of[at] = pivot if i % TILE == 0 else jnp.where(row == i % TILE, pivot, pivot_of[at])
                if i == GROUP - 1:
                    continue
                inverse = 1.0 / pivot
                below = dict(cols[i])
                below[at] = jnp.where(row > i % TILE, below[at], 0.0)
                factor = {t: below[t] * inverse for t in below}
                for k in range(i + 1, first + BLOCK):
                    across = spread(cols[i], k)
                    for t in cols[k]:
                        if k == i + 1:
                            cols[k][t] = cols[k][t] - (below[t] * across) * inverse
                        else:
                            cols[k][t] = cols[k][t] - factor[t] * across
                for side in sides:
                    across = spread(side, i)
                    for t in below:
                        side[t] = side[t] - factor[t] * across
    rows = slice(start, start + GROUP)
    rest = slice(start + GROUP, n)
    for state, sides, pivot_of in zip(states, halves, pivots):
        scale = jnp.concatenate([lax.rsqrt(p) for p in pivot_of], axis=0)
        left, right = [jnp.concatenate(side, axis=0) * scale for side in sides]
        state[rows, :n] = left
        state[rows, n:] = right
        if start + GROUP < n:
            lhs = split3(left)
            rhs = [jnp.concatenate(pair, axis=1) for pair in zip(lhs, split3(right))]
            state[rest, :] = state[rest, :] - deep_dot(lhs, rhs, TN)[rest, :]


def upper_blocks(size, n):
    count = size // n
    return [(i, j) for i in range(count) for j in range(i, count)]


def axis_bits(axis):
    size = lax.axis_size(axis)
    assert size & (size - 1) == 0, axis
    return [(axis, 1 << b) for b in range(size.bit_length() - 1)]


def plane_groups():
    first, *rest = axis_bits("gy") + axis_bits("gz")
    return [[first]] + [rest[b : b + 2] for b in range(0, len(rest), 2)]


def place_in(bits):
    place = 0
    for axis, distance in bits:
        place = place * 2 + lax.bitwise_and(lax.axis_index(axis) // distance, 1)
    return place


def plane_place():
    return place_in(sum(plane_groups(), []))


def fiber_place():
    return lax.axis_index("af")


def pick_kernel(distances, owner_ref, slab_ref, *pieces):
    width = pieces[0].shape[1]
    me = fiber_place()
    for distance, piece in zip(distances, pieces):
        block = 0
        for b in range(owner_ref.shape[-1]):
            block = jnp.where(owner_ref[0, 0, b] == lax.bitwise_xor(me, distance), b, block)
        piece[...] = slab_ref[:, pl.ds(pl.multiple_of(block * width, width), width)]


def pick_blocks(distances, owners, slab, **params):
    piece = jax.ShapeDtypeStruct((slab.shape[0], slab.shape[1] // owners.shape[-1]), slab.dtype)
    picked = pl.pallas_call(
        functools.partial(pick_kernel, distances),
        out_shape=(piece,) * len(distances),
        in_specs=[pl.BlockSpec(memory_space=pltpu.SMEM), pl.BlockSpec(memory_space=pltpu.VMEM)],
        compiler_params=pltpu.CompilerParams(**params),
        name="pick_blocks",
    )(owners, slab)
    return dict(zip(distances, picked))


def in_row_order(pieces, columns):
    rows = pieces[0].shape[0]
    me = fiber_place()
    for distance, piece in enumerate(pieces):
        start = pl.multiple_of(lax.bitwise_xor(me, distance) * rows, rows)
        columns[pl.ds(start, rows), :] = piece[...]


def gram_kernel(divisor, n, chunks, *refs):
    pieces, (kept_ref, sent_ref, columns, blocks) = refs[:-4], refs[-4:]
    in_row_order(pieces, columns)
    for b, (i, j) in enumerate(upper_blocks(columns.shape[0], n)):
        product = dot(columns[i * n : (i + 1) * n, :], columns[j * n : (j + 1) * n, :], NT)
        blocks[b * n : (b + 1) * n, :] = product / divisor
    place = plane_place()
    rows = blocks.shape[0] // chunks
    for slot in range(chunks):
        start = pl.multiple_of(lax.bitwise_xor(place, slot) * rows, rows)
        target = kept_ref if slot < chunks // 2 else sent_ref
        at = slot % (chunks // 2) * rows
        target[at : at + rows, :] = blocks[pl.ds(start, rows), :]


def local_gram(pieces, divisor, n, chunks):
    rows, width = pieces[0].shape
    size = rows * len(pieces)
    total = len(upper_blocks(size, n)) * n
    half = jax.ShapeDtypeStruct((total // 2, n), jnp.float32)
    return pl.pallas_call(
        functools.partial(gram_kernel, divisor, n, chunks),
        out_shape=(half, half),
        scratch_shapes=[pltpu.VMEM((size, width), pieces[0].dtype), pltpu.VMEM((total, n), jnp.float32)],
        compiler_params=pltpu.CompilerParams(vmem_limit_bytes=32 * 1024 * 1024),
        name="local_gram",
    )(*pieces)


def factor_kernel(chunks, fibers, *refs):
    slots, refs = refs[: chunks // 2], refs[chunks // 2 :]
    other_ref, basis_ref, refs = refs[0], refs[1], refs[2:]
    pieces, refs = refs[:fibers], refs[fibers:]
    tri_ref, out_ref, core_ref, blocks_ref, columns, high, middle, lower, work, one, two = refs
    size = tri_ref.shape[0]
    n = basis_ref.shape[1]
    in_row_order(pieces, columns)
    place = plane_place()
    rows = slots[0].shape[0]
    for slot in range(chunks):
        start = pl.multiple_of(lax.bitwise_xor(place, slot) * rows, rows)
        at = slot % (chunks // 2)
        if slot < chunks // 2:
            blocks_ref[pl.ds(start, rows), :] = slots[at][...]
        else:
            blocks_ref[pl.ds(start, rows), :] = other_ref[at * rows : (at + 1) * rows, :]
    phases = size // n
    part = [slice(i * n, (i + 1) * n) for i in range(phases)]
    for b, (i, j) in enumerate(upper_blocks(size, n)):
        block = blocks_ref[b * n : (b + 1) * n, :]
        work[part[i], part[j]] = block
        for ref, piece in zip((high, middle, lower), split3(block)):
            ref[part[i], part[j]] = piece
            if i != j:
                ref[part[j], part[i]] = piece.T
        if i != j:
            tri_ref[part[i], part[j]] = jnp.zeros((n, n), jnp.float32)
    eye = (
        lax.broadcasted_iota(jnp.int32, (n, n), 0) == lax.broadcasted_iota(jnp.int32, (n, n), 1)
    ).astype(jnp.float32)
    upper = lax.broadcasted_iota(jnp.int32, (n, n), 0) <= lax.broadcasted_iota(jnp.int32, (n, n), 1)
    basis = basis_ref[...]
    for phase in range(max(phases, 2 * ITERS)):
        if phase < phases:
            at = part[phase]
            one[:, :n] = work[at, at]
            one[:, n:] = eye
        if phase < 2 * ITERS:
            if phase % 2 == 0:
                parts = split3(basis)
                wide = split3(wide_dot((high[...], middle[...], lower[...]), parts, NN))
                two[:, :n] = wide_dot(parts, wide, TN)
            else:
                wide = split3(wide)
                two[:, :n] = wide_dot(wide, wide, TN)
            two[:, n:] = eye

        states = [one] * (phase < phases) + [two] * (phase < 2 * ITERS)
        for group in range(n // GROUP):
            eliminate(states, group * GROUP, n)
        if phase < phases:
            tri_ref[at, at] = jnp.where(upper, one[:, :n], 0.0).T
            if phase < phases - 1:
                rest = slice((phase + 1) * n, size)
                panel = deep_dot(split3(one[:, n:]), split3(work[at, rest]), NN)
                tri_ref[rest, at] = panel.T
                pieces = split3(panel)
                for i in range(phase + 1, phases):
                    tail = slice((i - phase - 1) * n, None)
                    mine = slice((i - phase - 1) * n, (i - phase) * n)
                    work[part[i], i * n :] = work[part[i], i * n :] - deep_dot(
                        [x[:, mine] for x in pieces], [x[:, tail] for x in pieces], TN
                    )
        if phase < 2 * ITERS:
            wide = short_dot(wide, split3(two[:, n:]), NT)
            if phase % 2 == 1:
                basis = wide
    out_ref[...] = basis
    core_ref[...] = dot(basis.astype(jnp.bfloat16), columns[...], TN).astype(jnp.bfloat16)


def factor(slots, other, basis, pieces):
    size, n = basis.shape
    width = pieces[0].shape[1]
    chunks = 2 * len(slots)
    return pl.pallas_call(
        functools.partial(factor_kernel, chunks, len(pieces)),
        out_shape=(
            jax.ShapeDtypeStruct((size, size), jnp.float32),
            jax.ShapeDtypeStruct((size, n), jnp.float32),
            jax.ShapeDtypeStruct((n, width), jnp.bfloat16),
        ),
        scratch_shapes=[
            pltpu.VMEM((2 * other.shape[0], n), jnp.float32),
            pltpu.VMEM((size, width), jnp.bfloat16),
            pltpu.VMEM((size, size), jnp.bfloat16),
            pltpu.VMEM((size, size), jnp.bfloat16),
            pltpu.VMEM((size, size), jnp.bfloat16),
            pltpu.VMEM((size, size), jnp.float32),
            pltpu.VMEM((n, 2 * n), jnp.float32),
            pltpu.VMEM((n, 2 * n), jnp.float32),
        ],
        compiler_params=pltpu.CompilerParams(vmem_limit_bytes=32 * 1024 * 1024),
        name="factor",
    )(*slots, other, basis, *pieces)


def swap(value, bits, change):
    axes = tuple(dict.fromkeys(axis for axis, _ in bits))
    sizes = [lax.axis_size(axis) for axis in axes]
    pairs = []
    for source, place in enumerate(np.ndindex(*sizes)):
        place = list(place)
        for b, (axis, distance) in enumerate(reversed(bits)):
            if (change >> b) & 1:
                place[axes.index(axis)] ^= distance
        pairs.append((source, int(np.ravel_multi_index(place, sizes))))
    return lax.ppermute(value, axes, pairs)


def sum_over_devices(kept, sent):
    first, *groups = plane_groups()
    value = kept + swap(sent, first, 1)
    for bits in groups:
        part = value.shape[0] >> len(bits)
        cuts = [value[d * part : (d + 1) * part] for d in range(1 << len(bits))]
        value = sum([swap(cuts[d], bits, d) for d in range(1, len(cuts))], cuts[0])
    for bit in axis_bits("af"):
        value = value + swap(value, [bit], 1)
    slots = [value]
    for bits in reversed(groups):
        whole = jnp.concatenate(slots, axis=0) if len(slots) > 1 else slots[0]
        slots = slots + [
            piece
            for d in range(1, 1 << len(bits))
            for piece in jnp.split(swap(whole, bits, d), len(slots), axis=0)
        ]
    return slots, swap(jnp.concatenate(slots, axis=0), first, 1)


def on_device(slab, block_owner, basis_init):
    fibers = lax.axis_size("af")
    chunks = lax.axis_size("gy") * lax.axis_size("gz")
    along = axis_bits("af")[::-1]
    far = fibers // 2
    pieces = pick_blocks([far], block_owner, slab)
    slab, _ = lax.optimization_barrier((slab, pieces[far]))
    others = [d for d in range(fibers) if d != far]
    pieces.update(pick_blocks(others, block_owner, slab, vmem_limit_bytes=8 * 1024 * 1024))
    pieces = [pieces[0]] + [swap(pieces[d], along, d) for d in range(1, fibers)]
    divisor = pieces[0].shape[1] * fibers * chunks
    kept, sent = local_gram(pieces, divisor, basis_init.shape[1], chunks)
    slots, other = sum_over_devices(kept, sent)
    return factor(slots, other, basis_init, pieces)


def solution(mesh):
    placed = (P("af", ("gy", "gz")), P("gy", "gz", None), P())
    return jax.shard_map(
        on_device,
        mesh=mesh,
        in_specs=placed,
        out_specs=(P(), P(), P(None, ("gy", "gz", "af"))),
        check_vma=False,
    )
```

```python
import functools

import jax
import jax.numpy as jnp
import numpy as np
from jax import lax
from jax.experimental import pallas as pl
from jax.experimental.pallas import tpu as pltpu
from jax.sharding import PartitionSpec as P

ITERS = 2
GROUP = 32
BLOCK = 16
TILE = 8


def split3(x):
    hi = x.astype(jnp.bfloat16)
    rest = x - hi.astype(jnp.float32)
    mid = rest.astype(jnp.bfloat16)
    low = (rest - mid.astype(jnp.float32)).astype(jnp.bfloat16)
    return hi, mid, low


def dot(a, b, dims):
    return lax.dot_general(a, b, (dims, ((), ())), preferred_element_type=jnp.float32)


NN, NT, TN = ((1,), (0,)), ((1,), (1,)), ((0,), (0,))


def deep_dot(a, b, dims):
    (ah, am, al), (bh, bm, bl) = a, b
    left = jnp.concatenate([ah, am, ah, am, ah, al], axis=dims[0][0])
    right = jnp.concatenate([bh, bh, bm, bm, bl, bh], axis=dims[1][0])
    return dot(left, right, dims)


def short_dot(a, b, dims):
    (ah, am, _), (bh, bm, _) = a, b
    left = jnp.concatenate([ah, am, ah], axis=dims[0][0])
    right = jnp.concatenate([bh, bh, bm], axis=dims[1][0])
    return dot(left, right, dims)


def wide_dot(a, b, dims):
    (ah, am, al), (bh, bm, bl) = a, b
    n = bh.shape[1]
    both = jnp.concatenate([bh, bm], axis=1)
    first = dot(ah, both, dims)
    second = dot(am, both, dims)
    small = dot(
        jnp.concatenate([ah, al], axis=dims[0][0]), jnp.concatenate([bl, bh], axis=0), dims
    )
    return first[:, :n] + (first[:, n:] + second[:, :n] + (second[:, n:] + small))


def eliminate(states, start, n):
    shape = (TILE, n)
    tiles = GROUP // TILE
    row = lax.broadcasted_iota(jnp.int32, shape, 0)

    def spread(value, i):
        return jnp.broadcast_to(value[i // TILE][i % TILE : i % TILE + 1, :], shape)

    halves = [
        [
            [state[start + t * TILE : start + (t + 1) * TILE, side] for t in range(tiles)]
            for side in (slice(0, n), slice(n, 2 * n))
        ]
        for state in states
    ]
    pivots = [[None] * tiles for _ in states]
    for first in range(0, GROUP, BLOCK):
        held = [
            {
                k: {
                    t: jnp.take_along_axis(left[t], jnp.full(shape, start + k, jnp.int32), axis=1, mode="promise_in_bounds")
                    for t in range(k // TILE, tiles)
                }
                for k in range(first, first + BLOCK)
            }
            for left, _ in halves
        ]
        for i in range(first, first + BLOCK):
            at = i // TILE
            for cols, sides, pivot_of in zip(held, halves, pivots):
                pivot = spread(cols[i], i)
                pivot_of[at] = pivot if i % TILE == 0 else jnp.where(row == i % TILE, pivot, pivot_of[at])
                if i == GROUP - 1:
                    continue
                inverse = 1.0 / pivot
                below = dict(cols[i])
                below[at] = jnp.where(row > i % TILE, below[at], 0.0)
                factor = {t: below[t] * inverse for t in below}
                for k in range(i + 1, first + BLOCK):
                    across = spread(cols[i], k)
                    for t in cols[k]:
                        if k == i + 1:
                            cols[k][t] = cols[k][t] - (below[t] * across) * inverse
                        else:
                            cols[k][t] = cols[k][t] - factor[t] * across
                for side in sides:
                    across = spread(side, i)
                    for t in below:
                        side[t] = side[t] - factor[t] * across
    rows = slice(start, start + GROUP)
    rest = slice(start + GROUP, n)
    for state, sides, pivot_of in zip(states, halves, pivots):
        scale = jnp.concatenate([lax.rsqrt(p) for p in pivot_of], axis=0)
        left, right = [jnp.concatenate(side, axis=0) * scale for side in sides]
        state[rows, :n] = left
        state[rows, n:] = right
        if start + GROUP < n:
            lhs = split3(left)
            rhs = [jnp.concatenate(pair, axis=1) for pair in zip(lhs, split3(right))]
            state[rest, :] = state[rest, :] - deep_dot(lhs, rhs, TN)[rest, :]


def upper_blocks(size, n):
    count = size // n
    return [(i, j) for i in range(count) for j in range(i, count)]


def summed_blocks(size, n, rows):
    return [(i, j) for i, j in upper_blocks(size, n) if i < j or rows != n]


def axis_bits(axis):
    size = lax.axis_size(axis)
    assert size & (size - 1) == 0, axis
    return [(axis, 1 << b) for b in range(size.bit_length() - 1)]


def plane_groups():
    first, *rest = axis_bits("gy") + axis_bits("gz")
    return [[first]] + [rest[b : b + 2] for b in range(0, len(rest), 2)]


def place_in(bits):
    place = 0
    for axis, distance in bits:
        place = place * 2 + lax.bitwise_and(lax.axis_index(axis) // distance, 1)
    return place


def plane_place():
    return place_in(sum(plane_groups(), []))


def fiber_place():
    return lax.axis_index("af")


def pick_kernel(distances, owner_ref, slab_ref, *pieces):
    width = pieces[0].shape[1]
    me = fiber_place()
    for distance, piece in zip(distances, pieces):
        block = 0
        for b in range(owner_ref.shape[-1]):
            block = jnp.where(owner_ref[0, 0, b] == lax.bitwise_xor(me, distance), b, block)
        piece[...] = slab_ref[:, pl.ds(pl.multiple_of(block * width, width), width)]


def pick_blocks(distances, owners, slab, **params):
    piece = jax.ShapeDtypeStruct((slab.shape[0], slab.shape[1] // owners.shape[-1]), slab.dtype)
    picked = pl.pallas_call(
        functools.partial(pick_kernel, distances),
        out_shape=(piece,) * len(distances),
        in_specs=[pl.BlockSpec(memory_space=pltpu.SMEM), pl.BlockSpec(memory_space=pltpu.VMEM)],
        compiler_params=pltpu.CompilerParams(**params),
        name="pick_blocks",
    )(owners, slab)
    return dict(zip(distances, picked))


def in_row_order(pieces, columns):
    rows = pieces[0].shape[0]
    me = fiber_place()
    for distance, piece in enumerate(pieces):
        start = pl.multiple_of(lax.bitwise_xor(me, distance) * rows, rows)
        columns[pl.ds(start, rows), :] = piece[...]


def gram_kernel(divisor, n, chunks, *refs):
    slab_ref, pieces, (kept_ref, sent_ref, columns, blocks, own) = refs[0], refs[1:-5], refs[-5:]
    in_row_order(pieces, columns)
    shared = summed_blocks(columns.shape[0], n, slab_ref.shape[0])
    for b, (i, j) in enumerate(shared):
        product = dot(columns[i * n : (i + 1) * n, :], columns[j * n : (j + 1) * n, :], NT)
        blocks[b * n : (b + 1) * n, :] = product / divisor
    parts = [blocks]
    if slab_ref.shape[0] == n:
        own[...] = dot(slab_ref[...], slab_ref[...], NT) / divisor
        parts.append(own)
    place = plane_place()
    rows = kept_ref.shape[0] // (chunks // 2)
    for slot in range(chunks):
        target = kept_ref if slot < chunks // 2 else sent_ref
        at = slot % (chunks // 2) * rows
        for part in parts:
            height = part.shape[0] // chunks
            start = pl.multiple_of(lax.bitwise_xor(place, slot) * height, height)
            target[at : at + height, :] = part[pl.ds(start, height), :]
            at += height


def local_gram(slab, pieces, divisor, n, chunks):
    rows, width = pieces[0].shape
    size = rows * len(pieces)
    total = len(summed_blocks(size, n, rows)) * n
    half = jax.ShapeDtypeStruct(((total + n * (rows == n)) // 2, n), jnp.float32)
    return pl.pallas_call(
        functools.partial(gram_kernel, divisor, n, chunks),
        out_shape=(half, half),
        scratch_shapes=[
            pltpu.VMEM((size, width), pieces[0].dtype),
            pltpu.VMEM((total, n), jnp.float32),
            pltpu.VMEM((n, n), jnp.float32),
        ],
        compiler_params=pltpu.CompilerParams(vmem_limit_bytes=16 * 1024 * 1024),
        name="local_gram",
    )(slab, *pieces)


def factor_kernel(chunks, fibers, *refs):
    slots, refs = refs[: chunks // 2], refs[chunks // 2 :]
    other_ref, basis_ref, refs = refs[0], refs[1], refs[2:]
    pieces, refs = refs[:fibers], refs[fibers:]
    tri_ref, out_ref, core_ref, blocks_ref, own_ref, columns, high, middle, lower, work, one, two = refs
    size = tri_ref.shape[0]
    n = basis_ref.shape[1]
    in_row_order(pieces, columns)
    place = plane_place()
    me = fiber_place()
    rows = slots[0].shape[0]
    height = blocks_ref.shape[0] // chunks
    own = n // chunks
    for slot in range(chunks):
        if slot < chunks // 2:
            chunk, at = slots[slot], 0
        else:
            chunk, at = other_ref, (slot - chunks // 2) * rows
        c = lax.bitwise_xor(place, slot)
        blocks_ref[pl.ds(pl.multiple_of(c * height, height), height), :] = chunk[at : at + height, :]
        for distance in range((rows - height) // own):
            start = pl.multiple_of(lax.bitwise_xor(me, distance) * n + c * own, own)
            low = at + height + distance * own
            own_ref[pl.ds(start, own), :] = chunk[low : low + own, :]
    phases = size // n
    part = [slice(i * n, (i + 1) * n) for i in range(phases)]
    shared = summed_blocks(size, n, pieces[0].shape[0])
    for i, j in upper_blocks(size, n):
        if (i, j) in shared:
            b = shared.index((i, j))
            block = blocks_ref[b * n : (b + 1) * n, :]
        else:
            block = own_ref[part[i], :]
        work[part[i], part[j]] = block
        for ref, piece in zip((high, middle, lower), split3(block)):
            ref[part[i], part[j]] = piece
            if i != j:
                ref[part[j], part[i]] = piece.T
        if i != j:
            tri_ref[part[i], part[j]] = jnp.zeros((n, n), jnp.float32)
    eye = (
        lax.broadcasted_iota(jnp.int32, (n, n), 0) == lax.broadcasted_iota(jnp.int32, (n, n), 1)
    ).astype(jnp.float32)
    upper = lax.broadcasted_iota(jnp.int32, (n, n), 0) <= lax.broadcasted_iota(jnp.int32, (n, n), 1)
    basis = basis_ref[...]
    for phase in range(max(phases, 2 * ITERS)):
        if phase < phases:
            at = part[phase]
            one[:, :n] = work[at, at]
            one[:, n:] = eye
        if phase < 2 * ITERS:
            if phase % 2 == 0:
                parts = split3(basis)
                wide = split3(wide_dot((high[...], middle[...], lower[...]), parts, NN))
                two[:, :n] = wide_dot(parts, wide, TN)
            else:
                wide = split3(wide)
                two[:, :n] = wide_dot(wide, wide, TN)
            two[:, n:] = eye

        states = [one] * (phase < phases) + [two] * (phase < 2 * ITERS)
        for group in range(n // GROUP):
            eliminate(states, group * GROUP, n)
        if phase < phases:
            tri_ref[at, at] = jnp.where(upper, one[:, :n], 0.0).T
            if phase < phases - 1:
                rest = slice((phase + 1) * n, size)
                panel = deep_dot(split3(one[:, n:]), split3(work[at, rest]), NN)
                tri_ref[rest, at] = panel.T
                pieces = split3(panel)
                for i in range(phase + 1, phases):
                    tail = slice((i - phase - 1) * n, None)
                    mine = slice((i - phase - 1) * n, (i - phase) * n)
                    work[part[i], i * n :] = work[part[i], i * n :] - deep_dot(
                        [x[:, mine] for x in pieces], [x[:, tail] for x in pieces], TN
                    )
        if phase < 2 * ITERS:
            wide = short_dot(wide, split3(two[:, n:]), NT)
            if phase % 2 == 1:
                basis = wide
    out_ref[...] = basis
    core_ref[...] = dot(basis.astype(jnp.bfloat16), columns[...], TN).astype(jnp.bfloat16)


def factor(slots, other, basis, pieces):
    size, n = basis.shape
    width = pieces[0].shape[1]
    chunks = 2 * len(slots)
    return pl.pallas_call(
        functools.partial(factor_kernel, chunks, len(pieces)),
        out_shape=(
            jax.ShapeDtypeStruct((size, size), jnp.float32),
            jax.ShapeDtypeStruct((size, n), jnp.float32),
            jax.ShapeDtypeStruct((n, width), jnp.bfloat16),
        ),
        scratch_shapes=[
            pltpu.VMEM((len(summed_blocks(size, n, pieces[0].shape[0])) * n, n), jnp.float32),
            pltpu.VMEM((size, n), jnp.float32),
            pltpu.VMEM((size, width), jnp.bfloat16),
            pltpu.VMEM((size, size), jnp.bfloat16),
            pltpu.VMEM((size, size), jnp.bfloat16),
            pltpu.VMEM((size, size), jnp.bfloat16),
            pltpu.VMEM((size, size), jnp.float32),
            pltpu.VMEM((n, 2 * n), jnp.float32),
            pltpu.VMEM((n, 2 * n), jnp.float32),
        ],
        compiler_params=pltpu.CompilerParams(vmem_limit_bytes=32 * 1024 * 1024),
        name="factor",
    )(*slots, other, basis, *pieces)


def swap(value, bits, change):
    axes = tuple(dict.fromkeys(axis for axis, _ in bits))
    sizes = [lax.axis_size(axis) for axis in axes]
    pairs = []
    for source, place in enumerate(np.ndindex(*sizes)):
        place = list(place)
        for b, (axis, distance) in enumerate(reversed(bits)):
            if (change >> b) & 1:
                place[axes.index(axis)] ^= distance
        pairs.append((source, int(np.ravel_multi_index(place, sizes))))
    return lax.ppermute(value, axes, pairs)


def sum_over_devices(kept, sent, own):
    first, *groups = plane_groups()
    value = kept + swap(sent, first, 1)
    for bits in groups:
        part = value.shape[0] >> len(bits)
        cuts = [value[d * part : (d + 1) * part] for d in range(1 << len(bits))]
        value = sum([swap(cuts[d], bits, d) for d in range(1, len(cuts))], cuts[0])
    height = value.shape[0] - own
    for bit in axis_bits("af"):
        got = swap(value, [bit], 1)
        value = jnp.concatenate([value[:height] + got[:height], value[height:], got[height:]], axis=0)
    slots = [value]
    for bits in reversed(groups):
        whole = jnp.concatenate(slots, axis=0) if len(slots) > 1 else slots[0]
        slots = slots + [
            piece
            for d in range(1, 1 << len(bits))
            for piece in jnp.split(swap(whole, bits, d), len(slots), axis=0)
        ]
    return slots, swap(jnp.concatenate(slots, axis=0), first, 1)


def on_device(slab, block_owner, basis_init):
    fibers = lax.axis_size("af")
    chunks = lax.axis_size("gy") * lax.axis_size("gz")
    along = axis_bits("af")[::-1]
    far = fibers // 2
    pieces = pick_blocks([far], block_owner, slab)
    slab, _ = lax.optimization_barrier((slab, pieces[far]))
    others = [d for d in range(fibers) if d != far]
    pieces.update(pick_blocks(others, block_owner, slab, vmem_limit_bytes=8 * 1024 * 1024))
    pieces = [pieces[0]] + [swap(pieces[d], along, d) for d in range(1, fibers)]
    divisor = pieces[0].shape[1] * fibers * chunks
    n = basis_init.shape[1]
    kept, sent = local_gram(slab, pieces, divisor, n, chunks)
    slots, other = sum_over_devices(kept, sent, n // chunks if slab.shape[0] == n else 0)
    return factor(slots, other, basis_init, pieces)


def solution(mesh):
    placed = (P("af", ("gy", "gz")), P("gy", "gz", None), P())
    return jax.shard_map(
        on_device,
        mesh=mesh,
        in_specs=placed,
        out_specs=(P(), P(), P(None, ("gy", "gz", "af"))),
        check_vma=False,
    )
```

```python
import functools

import jax
import jax.numpy as jnp
import numpy as np
from jax import lax
from jax.experimental import pallas as pl
from jax.experimental.pallas import tpu as pltpu
from jax.sharding import PartitionSpec as P

ITERS = 2
GROUP = 32
BLOCK = 16
TILE = 8


def split3(x):
    hi = x.astype(jnp.bfloat16)
    rest = x - hi.astype(jnp.float32)
    mid = rest.astype(jnp.bfloat16)
    low = (rest - mid.astype(jnp.float32)).astype(jnp.bfloat16)
    return hi, mid, low


def dot(a, b, dims):
    return lax.dot_general(a, b, (dims, ((), ())), preferred_element_type=jnp.float32)


NN, NT, TN = ((1,), (0,)), ((1,), (1,)), ((0,), (0,))


def deep_dot(a, b, dims):
    (ah, am, al), (bh, bm, bl) = a, b
    left = jnp.concatenate([ah, am, ah, am, ah, al], axis=dims[0][0])
    right = jnp.concatenate([bh, bh, bm, bm, bl, bh], axis=dims[1][0])
    return dot(left, right, dims)


def short_dot(a, b, dims):
    (ah, am, _), (bh, bm, _) = a, b
    left = jnp.concatenate([ah, am, ah], axis=dims[0][0])
    right = jnp.concatenate([bh, bh, bm], axis=dims[1][0])
    return dot(left, right, dims)


def wide_dot(a, b, dims):
    (ah, am, al), (bh, bm, bl) = a, b
    n = bh.shape[1]
    both = jnp.concatenate([bh, bm], axis=1)
    first = dot(ah, both, dims)
    second = dot(am, both, dims)
    small = dot(
        jnp.concatenate([ah, al], axis=dims[0][0]), jnp.concatenate([bl, bh], axis=0), dims
    )
    return first[:, :n] + (first[:, n:] + second[:, :n] + (second[:, n:] + small))


def eliminate(states, start, n):
    shape = (TILE, n)
    tiles = GROUP // TILE
    row = lax.broadcasted_iota(jnp.int32, shape, 0)

    def spread(value, i):
        return jnp.broadcast_to(value[i // TILE][i % TILE : i % TILE + 1, :], shape)

    halves = [
        [
            [state[start + t * TILE : start + (t + 1) * TILE, side] for t in range(tiles)]
            for side in (slice(0, n), slice(n, 2 * n))
        ]
        for state in states
    ]
    pivots = [[None] * tiles for _ in states]
    for first in range(0, GROUP, BLOCK):
        held = [
            {
                k: {
                    t: jnp.take_along_axis(left[t], jnp.full(shape, start + k, jnp.int32), axis=1, mode="promise_in_bounds")
                    for t in range(k // TILE, tiles)
                }
                for k in range(first, first + BLOCK)
            }
            for left, _ in halves
        ]
        for i in range(first, first + BLOCK):
            at = i // TILE
            for cols, sides, pivot_of in zip(held, halves, pivots):
                pivot = spread(cols[i], i)
                pivot_of[at] = pivot if i % TILE == 0 else jnp.where(row == i % TILE, pivot, pivot_of[at])
                if i == GROUP - 1:
                    continue
                inverse = 1.0 / pivot
                below = dict(cols[i])
                below[at] = jnp.where(row > i % TILE, below[at], 0.0)
                factor = {t: below[t] * inverse for t in below}
                for k in range(i + 1, first + BLOCK):
                    across = spread(cols[i], k)
                    for t in cols[k]:
                        if k == i + 1:
                            cols[k][t] = cols[k][t] - (below[t] * across) * inverse
                        else:
                            cols[k][t] = cols[k][t] - factor[t] * across
                for side in sides:
                    across = spread(side, i)
                    for t in below:
                        side[t] = side[t] - factor[t] * across
    rows = slice(start, start + GROUP)
    rest = slice(start + GROUP, n)
    for state, sides, pivot_of in zip(states, halves, pivots):
        scale = jnp.concatenate([lax.rsqrt(p) for p in pivot_of], axis=0)
        left, right = [jnp.concatenate(side, axis=0) * scale for side in sides]
        state[rows, :n] = left
        state[rows, n:] = right
        if start + GROUP < n:
            lhs = split3(left)
            rhs = [jnp.concatenate(pair, axis=1) for pair in zip(lhs, split3(right))]
            state[rest, :] = state[rest, :] - deep_dot(lhs, rhs, TN)[rest, :]


def upper_blocks(size, n):
    count = size // n
    return [(i, j) for i in range(count) for j in range(i, count)]


def summed_blocks(size, n, rows):
    return [(i, j) for i, j in upper_blocks(size, n) if i < j or rows != n]


def axis_bits(axis):
    size = lax.axis_size(axis)
    assert size & (size - 1) == 0, axis
    return [(axis, 1 << b) for b in range(size.bit_length() - 1)]


def plane_groups():
    first, *rest = axis_bits("gy") + axis_bits("gz")
    return [[first]] + [rest[b : b + 2] for b in range(0, len(rest), 2)]


def place_in(bits):
    place = 0
    for axis, distance in bits:
        place = place * 2 + lax.bitwise_and(lax.axis_index(axis) // distance, 1)
    return place


def plane_place():
    return place_in(sum(plane_groups(), []))


def fiber_place():
    return lax.axis_index("af")


def pick_kernel(distances, owner_ref, slab_ref, *pieces):
    width = pieces[0].shape[1]
    me = fiber_place()
    for distance, piece in zip(distances, pieces):
        block = 0
        for b in range(owner_ref.shape[-1]):
            block = jnp.where(owner_ref[0, 0, b] == lax.bitwise_xor(me, distance), b, block)
        piece[...] = slab_ref[:, pl.ds(pl.multiple_of(block * width, width), width)]


def pick_blocks(distances, owners, slab, **params):
    piece = jax.ShapeDtypeStruct((slab.shape[0], slab.shape[1] // owners.shape[-1]), slab.dtype)
    picked = pl.pallas_call(
        functools.partial(pick_kernel, distances),
        out_shape=(piece,) * len(distances),
        in_specs=[pl.BlockSpec(memory_space=pltpu.SMEM), pl.BlockSpec(memory_space=pltpu.VMEM)],
        compiler_params=pltpu.CompilerParams(**params),
        name="pick_blocks",
    )(owners, slab)
    return dict(zip(distances, picked))


def in_row_order(pieces, columns):
    rows = pieces[0].shape[0]
    me = fiber_place()
    for distance, piece in enumerate(pieces):
        start = pl.multiple_of(lax.bitwise_xor(me, distance) * rows, rows)
        columns[pl.ds(start, rows), :] = piece[...]


def gram_kernel(divisor, n, chunks, *refs):
    slab_ref, pieces, (kept_ref, sent_ref, columns, blocks, own) = refs[0], refs[1:-5], refs[-5:]
    in_row_order(pieces, columns)
    shared = summed_blocks(columns.shape[0], n, slab_ref.shape[0])
    for b, (i, j) in enumerate(shared):
        product = dot(columns[i * n : (i + 1) * n, :], columns[j * n : (j + 1) * n, :], NT)
        blocks[b * n : (b + 1) * n, :] = product / divisor
    parts = [blocks]
    if slab_ref.shape[0] == n:
        own[...] = dot(slab_ref[...], slab_ref[...], NT) / divisor
        parts.append(own)
    place = plane_place()
    rows = kept_ref.shape[0] // (chunks // 2)
    for slot in range(chunks):
        target = kept_ref if slot < chunks // 2 else sent_ref
        at = slot % (chunks // 2) * rows
        for part in parts:
            height = part.shape[0] // chunks
            start = pl.multiple_of(lax.bitwise_xor(place, slot) * height, height)
            target[at : at + height, :] = part[pl.ds(start, height), :]
            at += height


def local_gram(slab, pieces, divisor, n, chunks):
    rows, width = pieces[0].shape
    size = rows * len(pieces)
    total = len(summed_blocks(size, n, rows)) * n
    half = jax.ShapeDtypeStruct(((total + n * (rows == n)) // 2, n), jnp.float32)
    return pl.pallas_call(
        functools.partial(gram_kernel, divisor, n, chunks),
        out_shape=(half, half),
        scratch_shapes=[
            pltpu.VMEM((size, width), pieces[0].dtype),
            pltpu.VMEM((total, n), jnp.float32),
            pltpu.VMEM((n, n), jnp.float32),
        ],
        compiler_params=pltpu.CompilerParams(vmem_limit_bytes=16 * 1024 * 1024),
        name="local_gram",
    )(slab, *pieces)


def factor_kernel(chunks, fibers, *refs):
    slots, refs = refs[: chunks // 2], refs[chunks // 2 :]
    other_ref, basis_ref, refs = refs[0], refs[1], refs[2:]
    pieces, refs = refs[:fibers], refs[fibers:]
    tri_ref, out_ref, core_ref, blocks_ref, own_ref, columns, high, middle, lower, work, one, two = refs
    size = tri_ref.shape[0]
    n = basis_ref.shape[1]
    in_row_order(pieces, columns)
    place = plane_place()
    me = fiber_place()
    rows = slots[0].shape[0]
    height = blocks_ref.shape[0] // chunks
    own = n // chunks
    for slot in range(chunks):
        if slot < chunks // 2:
            chunk, at = slots[slot], 0
        else:
            chunk, at = other_ref, (slot - chunks // 2) * rows
        c = lax.bitwise_xor(place, slot)
        blocks_ref[pl.ds(pl.multiple_of(c * height, height), height), :] = chunk[at : at + height, :]
        for distance in range((rows - height) // own):
            start = pl.multiple_of(lax.bitwise_xor(me, distance) * n + c * own, own)
            low = at + height + distance * own
            own_ref[pl.ds(start, own), :] = chunk[low : low + own, :]
    phases = size // n
    part = [slice(i * n, (i + 1) * n) for i in range(phases)]
    shared = summed_blocks(size, n, pieces[0].shape[0])
    for i, j in upper_blocks(size, n):
        if (i, j) in shared:
            b = shared.index((i, j))
            block = blocks_ref[b * n : (b + 1) * n, :]
        else:
            block = own_ref[part[i], :]
        work[part[i], part[j]] = block
        for ref, piece in zip((high, middle, lower), split3(block)):
            ref[part[i], part[j]] = piece
            if i != j:
                ref[part[j], part[i]] = piece.T
        if i != j:
            tri_ref[part[i], part[j]] = jnp.zeros((n, n), jnp.float32)
    eye = (
        lax.broadcasted_iota(jnp.int32, (n, n), 0) == lax.broadcasted_iota(jnp.int32, (n, n), 1)
    ).astype(jnp.float32)
    upper = lax.broadcasted_iota(jnp.int32, (n, n), 0) <= lax.broadcasted_iota(jnp.int32, (n, n), 1)
    basis = basis_ref[...]
    for phase in range(max(phases, 2 * ITERS)):
        if phase < phases:
            at = part[phase]
            one[:, :n] = work[at, at]
            one[:, n:] = eye
        if phase < 2 * ITERS:
            if phase % 2 == 0:
                parts = split3(basis)
                wide = split3(wide_dot((high[...], middle[...], lower[...]), parts, NN))
                two[:, :n] = wide_dot(parts, wide, TN)
            else:
                wide = split3(wide)
                two[:, :n] = wide_dot(wide, wide, TN)
            two[:, n:] = eye

        states = [one] * (phase < phases) + [two] * (phase < 2 * ITERS)
        for group in range(n // GROUP):
            eliminate(states, group * GROUP, n)
        if phase < phases:
            tri_ref[at, at] = jnp.where(upper, one[:, :n], 0.0).T
            if phase < phases - 1:
                rest = slice((phase + 1) * n, size)
                panel = deep_dot(split3(one[:, n:]), split3(work[at, rest]), NN)
                tri_ref[rest, at] = panel.T
                pieces = split3(panel)
                for i in range(phase + 1, phases):
                    tail = slice((i - phase - 1) * n, None)
                    mine = slice((i - phase - 1) * n, (i - phase) * n)
                    work[part[i], i * n :] = work[part[i], i * n :] - deep_dot(
                        [x[:, mine] for x in pieces], [x[:, tail] for x in pieces], TN
                    )
        if phase < 2 * ITERS:
            wide = short_dot(wide, split3(two[:, n:]), NT)
            if phase % 2 == 1:
                basis = wide
    out_ref[...] = basis
    core_ref[...] = dot(basis.astype(jnp.bfloat16), columns[...], TN).astype(jnp.bfloat16)


def factor(slots, other, basis, pieces):
    size, n = basis.shape
    width = pieces[0].shape[1]
    chunks = 2 * len(slots)
    return pl.pallas_call(
        functools.partial(factor_kernel, chunks, len(pieces)),
        out_shape=(
            jax.ShapeDtypeStruct((size, size), jnp.float32),
            jax.ShapeDtypeStruct((size, n), jnp.float32),
            jax.ShapeDtypeStruct((n, width), jnp.bfloat16),
        ),
        scratch_shapes=[
            pltpu.VMEM((len(summed_blocks(size, n, pieces[0].shape[0])) * n, n), jnp.float32),
            pltpu.VMEM((size, n), jnp.float32),
            pltpu.VMEM((size, width), jnp.bfloat16),
            pltpu.VMEM((size, size), jnp.bfloat16),
            pltpu.VMEM((size, size), jnp.bfloat16),
            pltpu.VMEM((size, size), jnp.bfloat16),
            pltpu.VMEM((size, size), jnp.float32),
            pltpu.VMEM((n, 2 * n), jnp.float32),
            pltpu.VMEM((n, 2 * n), jnp.float32),
        ],
        compiler_params=pltpu.CompilerParams(vmem_limit_bytes=32 * 1024 * 1024),
        name="factor",
    )(*slots, other, basis, *pieces)


def swap(value, bits, change):
    axes = tuple(dict.fromkeys(axis for axis, _ in bits))
    sizes = [lax.axis_size(axis) for axis in axes]
    pairs = []
    for source, place in enumerate(np.ndindex(*sizes)):
        place = list(place)
        for b, (axis, distance) in enumerate(reversed(bits)):
            if (change >> b) & 1:
                place[axes.index(axis)] ^= distance
        pairs.append((source, int(np.ravel_multi_index(place, sizes))))
    return lax.ppermute(value, axes, pairs)


def sum_over_devices(kept, sent, own):
    first, *groups = plane_groups()
    value = kept + swap(sent, first, 1)
    for bits in groups:
        part = value.shape[0] >> len(bits)
        cuts = [value[d * part : (d + 1) * part] for d in range(1 << len(bits))]
        value = sum([swap(cuts[d], bits, d) for d in range(1, len(cuts))], cuts[0])
    height = value.shape[0] - own
    along = axis_bits("af")
    for bits in [along[b : b + 2][::-1] for b in range(0, len(along), 2)]:
        got = [swap(value, bits, d) for d in range(1, 1 << len(bits))]
        summed = sum([piece[:height] for piece in got], value[:height])
        value = jnp.concatenate([summed, value[height:]] + [piece[height:] for piece in got], axis=0)
    slots = [value]
    for bits in reversed(groups):
        whole = jnp.concatenate(slots, axis=0) if len(slots) > 1 else slots[0]
        slots = slots + [
            piece
            for d in range(1, 1 << len(bits))
            for piece in jnp.split(swap(whole, bits, d), len(slots), axis=0)
        ]
    return slots, swap(jnp.concatenate(slots, axis=0), first, 1)


def on_device(slab, block_owner, basis_init):
    fibers = lax.axis_size("af")
    chunks = lax.axis_size("gy") * lax.axis_size("gz")
    along = axis_bits("af")[::-1]
    far = fibers // 2
    pieces = pick_blocks([far], block_owner, slab)
    slab, _ = lax.optimization_barrier((slab, pieces[far]))
    others = [d for d in range(fibers) if d != far]
    pieces.update(pick_blocks(others, block_owner, slab, vmem_limit_bytes=8 * 1024 * 1024))
    pieces = [pieces[0]] + [swap(pieces[d], along, d) for d in range(1, fibers)]
    divisor = pieces[0].shape[1] * fibers * chunks
    n = basis_init.shape[1]
    kept, sent = local_gram(slab, pieces, divisor, n, chunks)
    slots, other = sum_over_devices(kept, sent, n // chunks if slab.shape[0] == n else 0)
    return factor(slots, other, basis_init, pieces)


def solution(mesh):
    placed = (P("af", ("gy", "gz")), P("gy", "gz", None), P())
    return jax.shard_map(
        on_device,
        mesh=mesh,
        in_specs=placed,
        out_specs=(P(), P(), P(None, ("gy", "gz", "af"))),
        check_vma=False,
    )
```

```python
import functools

import jax
import jax.numpy as jnp
import numpy as np
from jax import lax
from jax.experimental import pallas as pl
from jax.experimental.pallas import tpu as pltpu
from jax.sharding import PartitionSpec as P

ITERS = 2
GROUP = 32
BLOCK = 16
LIMIT = 2500.0
TILE = 8


def split3(x):
    hi = x.astype(jnp.bfloat16)
    rest = x - hi.astype(jnp.float32)
    mid = rest.astype(jnp.bfloat16)
    low = (rest - mid.astype(jnp.float32)).astype(jnp.bfloat16)
    return hi, mid, low


def dot(a, b, dims):
    return lax.dot_general(a, b, (dims, ((), ())), preferred_element_type=jnp.float32)


NN, NT, TN = ((1,), (0,)), ((1,), (1,)), ((0,), (0,))


def deep_dot(a, b, dims):
    (ah, am, al), (bh, bm, bl) = a, b
    left = jnp.concatenate([ah, am, ah, am, ah, al], axis=dims[0][0])
    right = jnp.concatenate([bh, bh, bm, bm, bl, bh], axis=dims[1][0])
    return dot(left, right, dims)


def short_dot(a, b, dims):
    (ah, am, _), (bh, bm, _) = a, b
    left = jnp.concatenate([ah, am, ah], axis=dims[0][0])
    right = jnp.concatenate([bh, bh, bm], axis=dims[1][0])
    return dot(left, right, dims)


def wide_dot(a, b, dims):
    (ah, am, al), (bh, bm, bl) = a, b
    n = bh.shape[1]
    both = jnp.concatenate([bh, bm], axis=1)
    first = dot(ah, both, dims)
    second = dot(am, both, dims)
    small = dot(
        jnp.concatenate([ah, al], axis=dims[0][0]), jnp.concatenate([bl, bh], axis=0), dims
    )
    return first[:, :n] + (first[:, n:] + second[:, :n] + (second[:, n:] + small))


def rows_of(start, size):
    if isinstance(start, int):
        return slice(start, start + size)
    return pl.ds(pl.multiple_of(start, TILE), size)


def eliminate(states, start, n):
    shape = (TILE, n)
    tiles = GROUP // TILE
    row = lax.broadcasted_iota(jnp.int32, shape, 0)

    def spread(value, i):
        return jnp.broadcast_to(value[i // TILE][i % TILE : i % TILE + 1, :], shape)

    halves = [
        [
            [state[rows_of(start + t * TILE, TILE), side] for t in range(tiles)]
            for side in (slice(0, n), slice(n, 2 * n))
        ]
        for state in states
    ]
    pivots = [[None] * tiles for _ in states]
    for first in range(0, GROUP, BLOCK):
        held = [
            {
                k: {
                    t: jnp.take_along_axis(left[t], jnp.full(shape, start + k, jnp.int32), axis=1, mode="promise_in_bounds")
                    for t in range(k // TILE, tiles)
                }
                for k in range(first, first + BLOCK)
            }
            for left, _ in halves
        ]
        for i in range(first, first + BLOCK):
            at = i // TILE
            for cols, sides, pivot_of in zip(held, halves, pivots):
                pivot = spread(cols[i], i)
                pivot_of[at] = pivot if i % TILE == 0 else jnp.where(row == i % TILE, pivot, pivot_of[at])
                if i == GROUP - 1:
                    continue
                inverse = 1.0 / pivot
                below = dict(cols[i])
                below[at] = jnp.where(row > i % TILE, below[at], 0.0)
                factor = {t: below[t] * inverse for t in below}
                for k in range(i + 1, first + BLOCK):
                    across = spread(cols[i], k)
                    for t in cols[k]:
                        if k == i + 1:
                            cols[k][t] = cols[k][t] - (below[t] * across) * inverse
                        else:
                            cols[k][t] = cols[k][t] - factor[t] * across
                for side in sides:
                    across = spread(side, i)
                    for t in below:
                        side[t] = side[t] - factor[t] * across
    rows = rows_of(start, GROUP)
    lane = lax.broadcasted_iota(jnp.int32, (GROUP, n), 1)
    for state, sides, pivot_of in zip(states, halves, pivots):
        scale = jnp.concatenate([lax.rsqrt(p) for p in pivot_of], axis=0)
        left, right = [jnp.concatenate(side, axis=0) * scale for side in sides]
        state[rows, :n] = left
        state[rows, n:] = right
        lhs = split3(left)
        rhs = [jnp.concatenate(pair, axis=1) for pair in zip(lhs, split3(right))]
        if not isinstance(start, int):
            lhs = [jnp.where(lane >= start + GROUP, x, jnp.zeros_like(x)) for x in lhs]
            state[...] = state[...] - deep_dot(lhs, rhs, TN)
        elif start + GROUP < n:
            rest = slice(start + GROUP, n)
            state[rest, :] = state[rest, :] - deep_dot(lhs, rhs, TN)[rest, :]


def upper_blocks(size, n):
    count = size // n
    return [(i, j) for i in range(count) for j in range(i, count)]


def summed_blocks(size, n, rows):
    return [(i, j) for i, j in upper_blocks(size, n) if i < j or rows != n]


def axis_bits(axis):
    size = lax.axis_size(axis)
    assert size & (size - 1) == 0, axis
    return [(axis, 1 << b) for b in range(size.bit_length() - 1)]


def plane_groups():
    first, *rest = axis_bits("gy") + axis_bits("gz")
    return [[first]] + [rest[b : b + 2] for b in range(0, len(rest), 2)]


def place_in(bits):
    place = 0
    for axis, distance in bits:
        place = place * 2 + lax.bitwise_and(lax.axis_index(axis) // distance, 1)
    return place


def plane_place():
    return place_in(sum(plane_groups(), []))


def fiber_place():
    return lax.axis_index("af")


def pick_kernel(distances, owner_ref, slab_ref, *pieces):
    width = pieces[0].shape[1]
    me = fiber_place()
    for distance, piece in zip(distances, pieces):
        block = 0
        for b in range(owner_ref.shape[-1]):
            block = jnp.where(owner_ref[0, 0, b] == lax.bitwise_xor(me, distance), b, block)
        piece[...] = slab_ref[:, pl.ds(pl.multiple_of(block * width, width), width)]


def pick_blocks(distances, owners, slab, **params):
    piece = jax.ShapeDtypeStruct((slab.shape[0], slab.shape[1] // owners.shape[-1]), slab.dtype)
    picked = pl.pallas_call(
        functools.partial(pick_kernel, distances),
        out_shape=(piece,) * len(distances),
        in_specs=[pl.BlockSpec(memory_space=pltpu.SMEM), pl.BlockSpec(memory_space=pltpu.VMEM)],
        compiler_params=pltpu.CompilerParams(**params),
        name="pick_blocks",
    )(owners, slab)
    return dict(zip(distances, picked))


def in_row_order(pieces, columns):
    rows = pieces[0].shape[0]
    me = fiber_place()
    for distance, piece in enumerate(pieces):
        start = pl.multiple_of(lax.bitwise_xor(me, distance) * rows, rows)
        columns[pl.ds(start, rows), :] = piece[...]


def gram_kernel(divisor, n, chunks, *refs):
    slab_ref, pieces, (kept_ref, sent_ref, columns, blocks, own) = refs[0], refs[1:-5], refs[-5:]
    in_row_order(pieces, columns)
    shared = summed_blocks(columns.shape[0], n, slab_ref.shape[0])
    for b, (i, j) in enumerate(shared):
        product = dot(columns[i * n : (i + 1) * n, :], columns[j * n : (j + 1) * n, :], NT)
        blocks[b * n : (b + 1) * n, :] = product / divisor
    parts = [blocks]
    if slab_ref.shape[0] == n:
        own[...] = dot(slab_ref[...], slab_ref[...], NT) / divisor
        parts.append(own)
    place = plane_place()
    rows = kept_ref.shape[0] // (chunks // 2)
    for slot in range(chunks):
        target = kept_ref if slot < chunks // 2 else sent_ref
        at = slot % (chunks // 2) * rows
        for part in parts:
            height = part.shape[0] // chunks
            start = pl.multiple_of(lax.bitwise_xor(place, slot) * height, height)
            target[at : at + height, :] = part[pl.ds(start, height), :]
            at += height


def local_gram(slab, pieces, divisor, n, chunks):
    rows, width = pieces[0].shape
    size = rows * len(pieces)
    total = len(summed_blocks(size, n, rows)) * n
    half = jax.ShapeDtypeStruct(((total + n * (rows == n)) // 2, n), jnp.float32)
    return pl.pallas_call(
        functools.partial(gram_kernel, divisor, n, chunks),
        out_shape=(half, half),
        scratch_shapes=[
            pltpu.VMEM((size, width), pieces[0].dtype),
            pltpu.VMEM((total, n), jnp.float32),
            pltpu.VMEM((n, n), jnp.float32),
        ],
        compiler_params=pltpu.CompilerParams(vmem_limit_bytes=16 * 1024 * 1024),
        name="local_gram",
    )(slab, *pieces)


def factor_kernel(chunks, fibers, *refs):
    slots, refs = refs[: chunks // 2], refs[chunks // 2 :]
    other_ref, basis_ref, refs = refs[0], refs[1], refs[2:]
    pieces, refs = refs[:fibers], refs[fibers:]
    tri_ref, out_ref, core_ref, blocks_ref, own_ref, columns, high, middle, lower, work, one, two, first = refs
    size = tri_ref.shape[0]
    n = basis_ref.shape[1]
    in_row_order(pieces, columns)
    place = plane_place()
    me = fiber_place()
    rows = slots[0].shape[0]
    height = blocks_ref.shape[0] // chunks
    own = n // chunks
    for slot in range(chunks):
        if slot < chunks // 2:
            chunk, at = slots[slot], 0
        else:
            chunk, at = other_ref, (slot - chunks // 2) * rows
        c = lax.bitwise_xor(place, slot)
        blocks_ref[pl.ds(pl.multiple_of(c * height, height), height), :] = chunk[at : at + height, :]
        for distance in range((rows - height) // own):
            start = pl.multiple_of(lax.bitwise_xor(me, distance) * n + c * own, own)
            low = at + height + distance * own
            own_ref[pl.ds(start, own), :] = chunk[low : low + own, :]
    phases = size // n
    part = [slice(i * n, (i + 1) * n) for i in range(phases)]
    shared = summed_blocks(size, n, pieces[0].shape[0])
    for i, j in upper_blocks(size, n):
        if (i, j) in shared:
            b = shared.index((i, j))
            block = blocks_ref[b * n : (b + 1) * n, :]
        else:
            block = own_ref[part[i], :]
        work[part[i], part[j]] = block
        for ref, piece in zip((high, middle, lower), split3(block)):
            ref[part[i], part[j]] = piece
            if i != j:
                ref[part[j], part[i]] = piece.T
        if i != j:
            tri_ref[part[i], part[j]] = jnp.zeros((n, n), jnp.float32)
    eye = (
        lax.broadcasted_iota(jnp.int32, (n, n), 0) == lax.broadcasted_iota(jnp.int32, (n, n), 1)
    ).astype(jnp.float32)
    upper = lax.broadcasted_iota(jnp.int32, (n, n), 0) <= lax.broadcasted_iota(jnp.int32, (n, n), 1)
    whole = (high, middle, lower)
    value = basis_ref[...]
    doubtful = jnp.zeros((1, 1), jnp.float32)
    for phase in range(max(phases, ITERS + 1)):
        if phase < phases:
            at = part[phase]
            one[:, :n] = work[at, at]
            one[:, n:] = eye
        if phase <= ITERS:
            pieces = split3(value)
            wide = split3(wide_dot([ref[...] for ref in whole], pieces, NN)) if phase < ITERS else pieces
            inner = wide_dot(pieces, wide, TN)
            two[:, :n] = inner
            two[:, n:] = eye
        states = [one] * (phase < phases) + [two] * (phase <= ITERS)
        for group in range(n // GROUP):
            eliminate(states, group * GROUP, n)
        if phase < phases:
            tri_ref[at, at] = jnp.where(upper, one[:, :n], 0.0).T
            if phase < phases - 1:
                rest = slice((phase + 1) * n, size)
                panel = deep_dot(split3(one[:, n:]), split3(work[at, rest]), NN)
                tri_ref[rest, at] = panel.T
                pieces = split3(panel)
                for i in range(phase + 1, phases):
                    tail = slice((i - phase - 1) * n, None)
                    mine = slice((i - phase - 1) * n, (i - phase) * n)
                    work[part[i], i * n :] = work[part[i], i * n :] - deep_dot(
                        [x[:, mine] for x in pieces], [x[:, tail] for x in pieces], TN
                    )
        if phase <= ITERS:
            if 0 < phase < ITERS:
                most = jnp.max(jnp.abs(two[:, n:]), axis=(0, 1), keepdims=True)
                spread = most * most * jnp.max(inner, axis=(0, 1), keepdims=True)
                doubtful = jnp.where(spread < LIMIT, doubtful, 1.0)
            value = short_dot(wide, split3(two[:, n:]), NT)
            if phase == 0:
                first[...] = value
    out_ref[...] = value

    @pl.when(doubtful[0, 0] > 0.0)
    def _():
        value = first[...]
        for half in range(1, 2 * ITERS):
            pieces = split3(value)
            wide = split3(wide_dot([ref[...] for ref in whole], pieces, NN)) if half % 2 == 0 else pieces
            two[:, :n] = wide_dot(pieces, wide, TN)
            two[:, n:] = eye

            def step(group, carry):
                eliminate([two], group * GROUP, n)
                return carry

            lax.fori_loop(0, n // GROUP, step, 0)
            value = short_dot(wide, split3(two[:, n:]), NT)
        out_ref[...] = value

    core_ref[...] = dot(out_ref[...].astype(jnp.bfloat16), columns[...], TN).astype(jnp.bfloat16)


def factor(slots, other, basis, pieces):
    size, n = basis.shape
    width = pieces[0].shape[1]
    chunks = 2 * len(slots)
    return pl.pallas_call(
        functools.partial(factor_kernel, chunks, len(pieces)),
        out_shape=(
            jax.ShapeDtypeStruct((size, size), jnp.float32),
            jax.ShapeDtypeStruct((size, n), jnp.float32),
            jax.ShapeDtypeStruct((n, width), jnp.bfloat16),
        ),
        scratch_shapes=[
            pltpu.VMEM((len(summed_blocks(size, n, pieces[0].shape[0])) * n, n), jnp.float32),
            pltpu.VMEM((size, n), jnp.float32),
            pltpu.VMEM((size, width), jnp.bfloat16),
            pltpu.VMEM((size, size), jnp.bfloat16),
            pltpu.VMEM((size, size), jnp.bfloat16),
            pltpu.VMEM((size, size), jnp.bfloat16),
            pltpu.VMEM((size, size), jnp.float32),
            pltpu.VMEM((n, 2 * n), jnp.float32),
            pltpu.VMEM((n, 2 * n), jnp.float32),
            pltpu.VMEM((size, n), jnp.float32),
        ],
        compiler_params=pltpu.CompilerParams(vmem_limit_bytes=32 * 1024 * 1024),
        name="factor",
    )(*slots, other, basis, *pieces)


def swap(value, bits, change):
    axes = tuple(dict.fromkeys(axis for axis, _ in bits))
    sizes = [lax.axis_size(axis) for axis in axes]
    pairs = []
    for source, place in enumerate(np.ndindex(*sizes)):
        place = list(place)
        for b, (axis, distance) in enumerate(reversed(bits)):
            if (change >> b) & 1:
                place[axes.index(axis)] ^= distance
        pairs.append((source, int(np.ravel_multi_index(place, sizes))))
    return lax.ppermute(value, axes, pairs)


def sum_over_devices(kept, sent, own):
    first, *groups = plane_groups()
    value = kept + swap(sent, first, 1)
    for bits in groups:
        part = value.shape[0] >> len(bits)
        cuts = [value[d * part : (d + 1) * part] for d in range(1 << len(bits))]
        value = sum([swap(cuts[d], bits, d) for d in range(1, len(cuts))], cuts[0])
    height = value.shape[0] - own
    along = axis_bits("af")
    for bits in [along[b : b + 2][::-1] for b in range(0, len(along), 2)]:
        got = [swap(value, bits, d) for d in range(1, 1 << len(bits))]
        summed = sum([piece[:height] for piece in got], value[:height])
        value = jnp.concatenate([summed, value[height:]] + [piece[height:] for piece in got], axis=0)
    slots = [value]
    for bits in reversed(groups):
        whole = jnp.concatenate(slots, axis=0) if len(slots) > 1 else slots[0]
        slots = slots + [
            piece
            for d in range(1, 1 << len(bits))
            for piece in jnp.split(swap(whole, bits, d), len(slots), axis=0)
        ]
    return slots, swap(jnp.concatenate(slots, axis=0), first, 1)


def on_device(slab, block_owner, basis_init):
    fibers = lax.axis_size("af")
    chunks = lax.axis_size("gy") * lax.axis_size("gz")
    along = axis_bits("af")[::-1]
    far = fibers // 2
    pieces = pick_blocks([far], block_owner, slab)
    slab, _ = lax.optimization_barrier((slab, pieces[far]))
    others = [d for d in range(fibers) if d != far]
    pieces.update(pick_blocks(others, block_owner, slab, vmem_limit_bytes=8 * 1024 * 1024))
    pieces = [pieces[0]] + [swap(pieces[d], along, d) for d in range(1, fibers)]
    divisor = pieces[0].shape[1] * fibers * chunks
    n = basis_init.shape[1]
    kept, sent = local_gram(slab, pieces, divisor, n, chunks)
    slots, other = sum_over_devices(kept, sent, n // chunks if slab.shape[0] == n else 0)
    return factor(slots, other, basis_init, pieces)


def solution(mesh):
    placed = (P("af", ("gy", "gz")), P("gy", "gz", None), P())
    return jax.shard_map(
        on_device,
        mesh=mesh,
        in_specs=placed,
        out_specs=(P(), P(), P(None, ("gy", "gz", "af"))),
        check_vma=False,
    )
```

```python
import functools

import jax
import jax.numpy as jnp
import numpy as np
from jax import lax
from jax.experimental import pallas as pl
from jax.experimental.pallas import tpu as pltpu
from jax.sharding import PartitionSpec as P

ITERS = 2
GROUP = 32
BLOCK = 16
LIMIT = 2500.0
TILE = 8


def split3(x):
    hi = x.astype(jnp.bfloat16)
    rest = x - hi.astype(jnp.float32)
    mid = rest.astype(jnp.bfloat16)
    low = (rest - mid.astype(jnp.float32)).astype(jnp.bfloat16)
    return hi, mid, low


def dot(a, b, dims):
    return lax.dot_general(a, b, (dims, ((), ())), preferred_element_type=jnp.float32)


NN, NT, TN = ((1,), (0,)), ((1,), (1,)), ((0,), (0,))


def deep_dot(a, b, dims):
    (ah, am, al), (bh, bm, bl) = a, b
    left = jnp.concatenate([ah, am, ah, am, ah, al], axis=dims[0][0])
    right = jnp.concatenate([bh, bh, bm, bm, bl, bh], axis=dims[1][0])
    return dot(left, right, dims)


def short_dot(a, b, dims):
    (ah, am, _), (bh, bm, _) = a, b
    left = jnp.concatenate([ah, am, ah], axis=dims[0][0])
    right = jnp.concatenate([bh, bh, bm], axis=dims[1][0])
    return dot(left, right, dims)


def wide_dot(a, b, dims):
    (ah, am, al), (bh, bm, bl) = a, b
    n = bh.shape[1]
    both = jnp.concatenate([bh, bm], axis=1)
    first = dot(ah, both, dims)
    second = dot(am, both, dims)
    small = dot(
        jnp.concatenate([ah, al], axis=dims[0][0]), jnp.concatenate([bl, bh], axis=0), dims
    )
    return first[:, :n] + (first[:, n:] + second[:, :n] + (second[:, n:] + small))


def rows_of(start, size):
    if isinstance(start, int):
        return slice(start, start + size)
    return pl.ds(pl.multiple_of(start, TILE), size)


def eliminate(states, start, n):
    shape = (TILE, n)
    tiles = GROUP // TILE
    row = lax.broadcasted_iota(jnp.int32, shape, 0)

    def spread(value, i):
        return jnp.broadcast_to(value[i // TILE][i % TILE : i % TILE + 1, :], shape)

    halves = [
        [
            [state[rows_of(start + t * TILE, TILE), side] for t in range(tiles)]
            for side in (slice(0, n), slice(n, 2 * n))
        ]
        for state in states
    ]
    pivots = [[None] * tiles for _ in states]
    for first in range(0, GROUP, BLOCK):
        held = [
            {
                k: {
                    t: jnp.take_along_axis(left[t], jnp.full(shape, start + k, jnp.int32), axis=1, mode="promise_in_bounds")
                    for t in range(k // TILE, tiles)
                }
                for k in range(first, first + BLOCK)
            }
            for left, _ in halves
        ]
        for i in range(first, first + BLOCK):
            at = i // TILE
            for cols, sides, pivot_of in zip(held, halves, pivots):
                pivot = spread(cols[i], i)
                pivot_of[at] = pivot if i % TILE == 0 else jnp.where(row == i % TILE, pivot, pivot_of[at])
                if i == GROUP - 1:
                    continue
                inverse = 1.0 / pivot
                below = dict(cols[i])
                below[at] = jnp.where(row > i % TILE, below[at], 0.0)
                factor = {t: below[t] * inverse for t in below}
                for k in range(i + 1, first + BLOCK):
                    across = spread(cols[i], k)
                    for t in cols[k]:
                        if k == i + 1:
                            cols[k][t] = cols[k][t] - (below[t] * across) * inverse
                        else:
                            cols[k][t] = cols[k][t] - factor[t] * across
                for side in sides:
                    across = spread(side, i)
                    for t in below:
                        side[t] = side[t] - factor[t] * across
    rows = rows_of(start, GROUP)
    lane = lax.broadcasted_iota(jnp.int32, (GROUP, n), 1)
    for state, sides, pivot_of in zip(states, halves, pivots):
        scale = jnp.concatenate([lax.rsqrt(p) for p in pivot_of], axis=0)
        left, right = [jnp.concatenate(side, axis=0) * scale for side in sides]
        state[rows, :n] = left
        state[rows, n:] = right
        lhs = split3(left)
        rhs = [jnp.concatenate(pair, axis=1) for pair in zip(lhs, split3(right))]
        if not isinstance(start, int):
            lhs = [jnp.where(lane >= start + GROUP, x, jnp.zeros_like(x)) for x in lhs]
            state[...] = state[...] - deep_dot(lhs, rhs, TN)
        elif start + GROUP < n:
            rest = slice(start + GROUP, n)
            state[rest, :] = state[rest, :] - deep_dot(lhs, rhs, TN)[rest, :]


def upper_blocks(size, n):
    count = size // n
    return [(i, j) for i in range(count) for j in range(i, count)]


def summed_blocks(size, n, rows):
    return [(i, j) for i, j in upper_blocks(size, n) if i < j or rows != n]


def axis_bits(axis):
    size = lax.axis_size(axis)
    assert size & (size - 1) == 0, axis
    return [(axis, 1 << b) for b in range(size.bit_length() - 1)]


def plane_groups():
    first, *rest = axis_bits("gy") + axis_bits("gz")
    return [[first]] + [rest[b : b + 2] for b in range(0, len(rest), 2)]


def place_in(bits):
    place = 0
    for axis, distance in bits:
        place = place * 2 + lax.bitwise_and(lax.axis_index(axis) // distance, 1)
    return place


def plane_place():
    return place_in(sum(plane_groups(), []))


def fiber_place():
    return lax.axis_index("af")


def pick_kernel(distances, owner_ref, slab_ref, *pieces):
    width = pieces[0].shape[1]
    me = fiber_place()
    for distance, piece in zip(distances, pieces):
        block = 0
        for b in range(owner_ref.shape[-1]):
            block = jnp.where(owner_ref[0, 0, b] == lax.bitwise_xor(me, distance), b, block)
        piece[...] = slab_ref[:, pl.ds(pl.multiple_of(block * width, width), width)]


def pick_blocks(distances, owners, slab, **params):
    piece = jax.ShapeDtypeStruct((slab.shape[0], slab.shape[1] // owners.shape[-1]), slab.dtype)
    picked = pl.pallas_call(
        functools.partial(pick_kernel, distances),
        out_shape=(piece,) * len(distances),
        in_specs=[pl.BlockSpec(memory_space=pltpu.SMEM), pl.BlockSpec(memory_space=pltpu.VMEM)],
        compiler_params=pltpu.CompilerParams(**params),
        name="pick_blocks",
    )(owners, slab)
    return dict(zip(distances, picked))


def in_row_order(pieces, columns):
    rows = pieces[0].shape[0]
    me = fiber_place()
    for distance, piece in enumerate(pieces):
        start = pl.multiple_of(lax.bitwise_xor(me, distance) * rows, rows)
        columns[pl.ds(start, rows), :] = piece[...]


def gram_kernel(divisor, n, chunks, *refs):
    slab_ref, pieces, (kept_ref, sent_ref, columns, blocks, own) = refs[0], refs[1:-5], refs[-5:]
    in_row_order(pieces, columns)
    shared = summed_blocks(columns.shape[0], n, slab_ref.shape[0])
    for b, (i, j) in enumerate(shared):
        product = dot(columns[i * n : (i + 1) * n, :], columns[j * n : (j + 1) * n, :], NT)
        blocks[b * n : (b + 1) * n, :] = product / divisor
    parts = [blocks]
    if slab_ref.shape[0] == n:
        own[...] = dot(slab_ref[...], slab_ref[...], NT) / divisor
        parts.append(own)
    place = plane_place()
    rows = kept_ref.shape[0] // (chunks // 2)
    for slot in range(chunks):
        target = kept_ref if slot < chunks // 2 else sent_ref
        at = slot % (chunks // 2) * rows
        for part in parts:
            height = part.shape[0] // chunks
            start = pl.multiple_of(lax.bitwise_xor(place, slot) * height, height)
            target[at : at + height, :] = part[pl.ds(start, height), :]
            at += height


def local_gram(slab, pieces, divisor, n, chunks):
    rows, width = pieces[0].shape
    size = rows * len(pieces)
    total = len(summed_blocks(size, n, rows)) * n
    half = jax.ShapeDtypeStruct(((total + n * (rows == n)) // 2, n), jnp.float32)
    return pl.pallas_call(
        functools.partial(gram_kernel, divisor, n, chunks),
        out_shape=(half, half),
        scratch_shapes=[
            pltpu.VMEM((size, width), pieces[0].dtype),
            pltpu.VMEM((total, n), jnp.float32),
            pltpu.VMEM((n, n), jnp.float32),
        ],
        compiler_params=pltpu.CompilerParams(vmem_limit_bytes=16 * 1024 * 1024),
        name="local_gram",
    )(slab, *pieces)


def factor_kernel(chunks, fibers, *refs):
    slots, refs = refs[: chunks // 2], refs[chunks // 2 :]
    other_ref, basis_ref, refs = refs[0], refs[1], refs[2:]
    pieces, refs = refs[:fibers], refs[fibers:]
    tri_ref, out_ref, core_ref, blocks_ref, own_ref, columns, high, middle, lower, work, one, two, first = refs
    size = tri_ref.shape[0]
    n = basis_ref.shape[1]
    in_row_order(pieces, columns)
    place = plane_place()
    me = fiber_place()
    rows = slots[0].shape[0]
    height = blocks_ref.shape[0] // chunks
    own = n // chunks
    for slot in range(chunks):
        if slot < chunks // 2:
            chunk, at = slots[slot], 0
        else:
            chunk, at = other_ref, (slot - chunks // 2) * rows
        c = lax.bitwise_xor(place, slot)
        blocks_ref[pl.ds(pl.multiple_of(c * height, height), height), :] = chunk[at : at + height, :]
        for distance in range((rows - height) // own):
            start = pl.multiple_of(lax.bitwise_xor(me, distance) * n + c * own, own)
            low = at + height + distance * own
            own_ref[pl.ds(start, own), :] = chunk[low : low + own, :]
    phases = size // n
    part = [slice(i * n, (i + 1) * n) for i in range(phases)]
    shared = summed_blocks(size, n, pieces[0].shape[0])
    for i, j in upper_blocks(size, n):
        if (i, j) in shared:
            b = shared.index((i, j))
            block = blocks_ref[b * n : (b + 1) * n, :]
        else:
            block = own_ref[part[i], :]
        work[part[i], part[j]] = block
        for ref, piece in zip((high, middle, lower), split3(block)):
            ref[part[i], part[j]] = piece
            if i != j:
                ref[part[j], part[i]] = piece.T
        if i != j:
            tri_ref[part[i], part[j]] = jnp.zeros((n, n), jnp.float32)
    eye = (
        lax.broadcasted_iota(jnp.int32, (n, n), 0) == lax.broadcasted_iota(jnp.int32, (n, n), 1)
    ).astype(jnp.float32)
    upper = lax.broadcasted_iota(jnp.int32, (n, n), 0) <= lax.broadcasted_iota(jnp.int32, (n, n), 1)
    whole = (high, middle, lower)
    value = basis_ref[...]

    def finish(basis):
        out_ref[...] = basis
        core_ref[...] = dot(basis.astype(jnp.bfloat16), columns[...], TN).astype(jnp.bfloat16)

    doubtful = jnp.zeros((1, 1), jnp.float32)
    for phase in range(max(phases, ITERS + 1)):
        if phase < phases:
            at = part[phase]
            one[:, :n] = work[at, at]
            one[:, n:] = eye
        if phase <= ITERS:
            pieces = split3(value)
            wide = split3(wide_dot([ref[...] for ref in whole], pieces, NN)) if phase < ITERS else pieces
            inner = wide_dot(pieces, wide, TN)
            two[:, :n] = inner
            two[:, n:] = eye
        states = [one] * (phase < phases) + [two] * (phase <= ITERS)
        for group in range(n // GROUP):
            eliminate(states, group * GROUP, n)
        if phase < phases:
            tri_ref[at, at] = jnp.where(upper, one[:, :n], 0.0).T
            if phase < phases - 1:
                rest = slice((phase + 1) * n, size)
                panel = deep_dot(split3(one[:, n:]), split3(work[at, rest]), NN)
                tri_ref[rest, at] = panel.T
                pieces = split3(panel)
                for i in range(phase + 1, phases):
                    tail = slice((i - phase - 1) * n, None)
                    mine = slice((i - phase - 1) * n, (i - phase) * n)
                    work[part[i], i * n :] = work[part[i], i * n :] - deep_dot(
                        [x[:, mine] for x in pieces], [x[:, tail] for x in pieces], TN
                    )
        if phase <= ITERS:
            if 0 < phase < ITERS:
                most = jnp.max(jnp.abs(two[:, n:]), axis=(0, 1), keepdims=True)
                spread = most * most * jnp.max(inner, axis=(0, 1), keepdims=True)
                doubtful = jnp.where(spread < LIMIT, doubtful, 1.0)
            value = short_dot(wide, split3(two[:, n:]), NT)
            if phase == 0:
                first[...] = value
            if phase == ITERS:
                finish(value)

    @pl.when(doubtful[0, 0] > 0.0)
    def _():
        value = first[...]
        for half in range(1, 2 * ITERS):
            pieces = split3(value)
            wide = split3(wide_dot([ref[...] for ref in whole], pieces, NN)) if half % 2 == 0 else pieces
            two[:, :n] = wide_dot(pieces, wide, TN)
            two[:, n:] = eye

            def step(group, carry):
                eliminate([two], group * GROUP, n)
                return carry

            lax.fori_loop(0, n // GROUP, step, 0)
            value = short_dot(wide, split3(two[:, n:]), NT)
        finish(value)


def factor(slots, other, basis, pieces):
    size, n = basis.shape
    width = pieces[0].shape[1]
    chunks = 2 * len(slots)
    return pl.pallas_call(
        functools.partial(factor_kernel, chunks, len(pieces)),
        out_shape=(
            jax.ShapeDtypeStruct((size, size), jnp.float32),
            jax.ShapeDtypeStruct((size, n), jnp.float32),
            jax.ShapeDtypeStruct((n, width), jnp.bfloat16),
        ),
        scratch_shapes=[
            pltpu.VMEM((len(summed_blocks(size, n, pieces[0].shape[0])) * n, n), jnp.float32),
            pltpu.VMEM((size, n), jnp.float32),
            pltpu.VMEM((size, width), jnp.bfloat16),
            pltpu.VMEM((size, size), jnp.bfloat16),
            pltpu.VMEM((size, size), jnp.bfloat16),
            pltpu.VMEM((size, size), jnp.bfloat16),
            pltpu.VMEM((size, size), jnp.float32),
            pltpu.VMEM((n, 2 * n), jnp.float32),
            pltpu.VMEM((n, 2 * n), jnp.float32),
            pltpu.VMEM((size, n), jnp.float32),
        ],
        compiler_params=pltpu.CompilerParams(vmem_limit_bytes=32 * 1024 * 1024),
        name="factor",
    )(*slots, other, basis, *pieces)


def swap(value, bits, change):
    axes = tuple(dict.fromkeys(axis for axis, _ in bits))
    sizes = [lax.axis_size(axis) for axis in axes]
    pairs = []
    for source, place in enumerate(np.ndindex(*sizes)):
        place = list(place)
        for b, (axis, distance) in enumerate(reversed(bits)):
            if (change >> b) & 1:
                place[axes.index(axis)] ^= distance
        pairs.append((source, int(np.ravel_multi_index(place, sizes))))
    return lax.ppermute(value, axes, pairs)


def sum_over_devices(kept, sent, own):
    first, *groups = plane_groups()
    value = kept + swap(sent, first, 1)
    for bits in groups:
        part = value.shape[0] >> len(bits)
        cuts = [value[d * part : (d + 1) * part] for d in range(1 << len(bits))]
        value = sum([swap(cuts[d], bits, d) for d in range(1, len(cuts))], cuts[0])
    height = value.shape[0] - own
    along = axis_bits("af")
    for bits in [along[b : b + 2][::-1] for b in range(0, len(along), 2)]:
        got = [swap(value, bits, d) for d in range(1, 1 << len(bits))]
        summed = sum([piece[:height] for piece in got], value[:height])
        value = jnp.concatenate([summed, value[height:]] + [piece[height:] for piece in got], axis=0)
    slots = [value]
    for bits in reversed(groups):
        whole = jnp.concatenate(slots, axis=0) if len(slots) > 1 else slots[0]
        slots = slots + [
            piece
            for d in range(1, 1 << len(bits))
            for piece in jnp.split(swap(whole, bits, d), len(slots), axis=0)
        ]
    return slots, swap(jnp.concatenate(slots, axis=0), first, 1)


def on_device(slab, block_owner, basis_init):
    fibers = lax.axis_size("af")
    chunks = lax.axis_size("gy") * lax.axis_size("gz")
    along = axis_bits("af")[::-1]
    far = fibers // 2
    pieces = pick_blocks([far], block_owner, slab)
    slab, _ = lax.optimization_barrier((slab, pieces[far]))
    others = [d for d in range(fibers) if d != far]
    pieces.update(pick_blocks(others, block_owner, slab, vmem_limit_bytes=8 * 1024 * 1024))
    pieces = [pieces[0]] + [swap(pieces[d], along, d) for d in range(1, fibers)]
    divisor = pieces[0].shape[1] * fibers * chunks
    n = basis_init.shape[1]
    kept, sent = local_gram(slab, pieces, divisor, n, chunks)
    slots, other = sum_over_devices(kept, sent, n // chunks if slab.shape[0] == n else 0)
    return factor(slots, other, basis_init, pieces)


def solution(mesh):
    placed = (P("af", ("gy", "gz")), P("gy", "gz", None), P())
    return jax.shard_map(
        on_device,
        mesh=mesh,
        in_specs=placed,
        out_specs=(P(), P(), P(None, ("gy", "gz", "af"))),
        check_vma=False,
    )
```
